32 devices in a mesh: dom: 8 (over z, core), rep: 4 (over y, x).
Axes of the slice: x: 2, y: 2, z: 4, core: 2. Of those that a mesh axis runs over, the one named last changes fastest.
Arguments:
- features: bfloat16 [8192, 512], P(('dom', 'rep')), may hold values from -6 to 6
- local_counts: int32 [8192, 256], P(('dom', 'rep')), may hold values from 0 to 3, as said below
- remote_counts: int32 [128, 128, 128], P(('dom', 'rep')), may hold values from 0 to 3, as said below
- remote_dest: int32 [32, 4], P(('dom', 'rep')), may hold values from 0 to 1
- send_block: int32 [32, 4], P(('dom', 'rep')), may hold values from 0 to 1
- halo_counts: int32 [64, 128, 128], P(('dom', 'rep')), may hold values from 0 to 3, as said below
- halo_dest: int32 [32, 2], P(('dom', 'rep')), may hold values from 0 to 1
- export_block: int32 [32, 1], P(('dom', 'rep')), may hold values from 0 to 1
- w_self: bfloat16 [512, 512], replicated, may hold values from -0.25 to 0.25
- w_neigh: bfloat16 [512, 512], replicated, may hold values from -0.25 to 0.25
- cotangent: bfloat16 [8192, 512], P(('dom', 'rep')), may hold values from -6 to 6
Outputs:
- output: bfloat16 [8192, 512], P(('dom', 'rep'))
- feature_grads: bfloat16 [8192, 512], P(('dom', 'rep'))
- self_grads: float32 [512, 512], replicated
- neigh_grads: float32 [512, 512], replicated
The draws below stay inside these ranges and needn't reach their ends.
Inputs may be any that keep to these rules, and one draw needn't show every extreme that they name: `local_counts`: edge counts of one destination row are 0 for isolated nodes and otherwise at most that row's level, a level of 1 to 3. `remote_counts`: as local_counts, with the level of the destination row. `halo_counts`: as local_counts; the entries for the previous partition of partition 0 and the next partition of the last partition are zero.
All inputs are finite; a program needn't handle non-finite values.
Results may differ from the reference program's by a relative error of at most 0.0051.
Values may be sent and summed in bfloat16 or wider, within the bound.
A program may use at most 64 MiB of HBM per device.

```python
import jax
import jax.numpy as jnp
from jax import lax

F = 512
BLK = 128
ROWS_DEV = 256
BPD = 2
NODES = 8192
N_DOM = 8
N_REP = 4


def layout_common(key):
    devices = N_DOM * N_REP
    blocks = ROWS_DEV // BLK
    keys = jax.random.split(key, 4)
    rarity = jax.random.randint(keys[0], (devices * ROWS_DEV,), 0, 32)
    level = jax.random.randint(keys[1], (devices * ROWS_DEV,), 1, 4)
    levels = jnp.where(rarity == 0, 0, level).astype(jnp.int32)
    remote_targets = jax.random.randint(keys[2], (devices, N_REP), 0, blocks).astype(jnp.int32)
    halo_targets = jax.random.randint(keys[3], (devices, 2), 0, blocks).astype(jnp.int32)
    return (levels, remote_targets, halo_targets)


def sparse_counts(key, shape, row_level, sparsity):
    first, second = jax.random.split(key)
    hits = jax.random.randint(first, shape, 0, sparsity) == 0
    value = jax.random.randint(second, shape, 1, 4)
    return jnp.where(hits, jnp.minimum(value, row_level), 0).astype(jnp.int32)


def draw_local_counts(key, part):
    levels, remote_targets, halo_targets = layout_common(key)
    key = jax.random.fold_in(key, 11)
    devices = N_DOM * N_REP
    return sparse_counts(key, (devices * ROWS_DEV, ROWS_DEV), levels[:, None], 64)


def draw_remote_counts(key, part):
    levels, remote_targets, halo_targets = layout_common(key)
    key = jax.random.fold_in(key, 23)
    devices = N_DOM * N_REP
    blocks = ROWS_DEV // BLK
    level_blocks = levels.reshape(devices, blocks, BLK)
    picked = jnp.take_along_axis(level_blocks, remote_targets[:, :, None], axis=1)
    return sparse_counts(key, (devices * N_REP, BLK, BLK), picked.reshape(devices * N_REP, BLK, 1), 32)


def draw_halo_counts(key, part):
    levels, remote_targets, halo_targets = layout_common(key)
    key = jax.random.fold_in(key, 37)
    devices = N_DOM * N_REP
    blocks = ROWS_DEV // BLK
    level_blocks = levels.reshape(devices, blocks, BLK)
    picked = jnp.take_along_axis(level_blocks, halo_targets[:, :, None], axis=1)
    group = jnp.arange(devices, dtype=jnp.int32) // N_REP
    keep = jnp.stack([group > 0, group < N_DOM - 1], axis=1).astype(jnp.int32)
    picked = picked * keep[:, :, None]
    return sparse_counts(key, (devices * 2, BLK, BLK), picked.reshape(devices * 2, BLK, 1), 16)


def draw_remote_dest(key, part):
    levels, remote_targets, halo_targets = layout_common(key)
    return remote_targets


def draw_halo_dest(key, part):
    levels, remote_targets, halo_targets = layout_common(key)
    return halo_targets


def place_ends(array, key, low, largest):
    longest = array.shape.index(max(array.shape))
    spots = []
    for shift in (0, 1):
        where = [jax.random.randint(jax.random.fold_in(key, axis), (), 0, length) for axis, length in enumerate(array.shape)]
        where[longest] = (where[longest] + shift) % array.shape[longest]
        spots.append(tuple(where))
    return array.at[spots[0]].set(low).at[spots[1]].set(largest)


def block_levels(rng, shape, cuts, low, largest):
    def one(position, blocks):
        steps = jax.random.uniform(jax.random.fold_in(jax.random.fold_in(rng, 6), position), (blocks,), jnp.float32, low / len(cuts), largest / len(cuts))
        return jnp.repeat(jnp.exp(steps), shape[position] // blocks).reshape((-1,) + (1,) * (len(shape) - position - 1))

    loudness = one(*cuts[0])
    for cut in cuts[1:]:
        loudness = loudness * one(*cut)
    return loudness


def normal_values(rng, shape, spread, most, cuts=(), kind=jnp.bfloat16):
    gain = block_levels(rng, shape, cuts, -0.22, 0.18) if cuts else 1.0
    result = jax.random.normal(rng, shape, jnp.float32) * spread * gain
    return jnp.minimum(jnp.maximum(result, -most), most).astype(kind)


def setup_inputs(seed: int = 0) -> dict:
    arg_keys = jax.random.split(jax.random.key(seed), 12)
    return {
        "features": normal_values(arg_keys[0], (NODES, F), 1.0, 6.0, ((0, 32),)),
        "local_counts": draw_local_counts(jax.random.fold_in(arg_keys[11], 71), 0),
        "remote_counts": draw_remote_counts(jax.random.fold_in(arg_keys[11], 71), 0),
        "remote_dest": draw_remote_dest(jax.random.fold_in(arg_keys[11], 71), 0),
        "send_block": place_ends(jax.random.randint(arg_keys[4], (N_DOM * N_REP, N_REP), 0, BPD), jax.random.fold_in(arg_keys[4], 1), 0, BPD - 1).astype(jnp.int32),
        "halo_counts": draw_halo_counts(jax.random.fold_in(arg_keys[11], 71), 0),
        "halo_dest": draw_halo_dest(jax.random.fold_in(arg_keys[11], 71), 0),
        "export_block": place_ends(jax.random.randint(arg_keys[7], (N_DOM * N_REP, 1), 0, BPD), jax.random.fold_in(arg_keys[7], 1), 0, BPD - 1).astype(jnp.int32),
        "w_self": normal_values(arg_keys[8], (F, F), F ** -0.5, 0.25),
        "w_neigh": normal_values(arg_keys[9], (F, F), F ** -0.5, 0.25),
        "cotangent": normal_values(arg_keys[10], (NODES, F), 1.0, 6.0, ((0, 32),)),
    }


def reference(features, local_counts, remote_counts, remote_dest, send_block, halo_counts, halo_dest, export_block, w_self, w_neigh, cotangent):
    devices = N_DOM * N_REP
    blocks = ROWS_DEV // BLK
    highest = lax.Precision.HIGHEST
    feat_blocks = features.reshape(devices, blocks, BLK, F)
    local_all = local_counts.reshape(devices, ROWS_DEV, ROWS_DEV)
    remote_all = remote_counts.reshape(devices, N_REP, BLK, BLK)
    halo_all = halo_counts.reshape(devices, 2, BLK, BLK)
    block_ids = jnp.arange(blocks, dtype=jnp.int32)
    members = jnp.arange(N_REP, dtype=jnp.int32)
    zero_block = jnp.zeros((BLK, F), jnp.bfloat16)

    def onehot(index):
        return (index[:, None] == block_ids[None, :]).astype(jnp.float32)

    def forward_device(device):
        group = device // N_REP
        member_index = device % N_REP
        peers = group * N_REP + members
        arrived = feat_blocks[peers, send_block[peers, member_index]]
        prev_dev = jnp.maximum(device - N_REP, 0)
        next_dev = jnp.minimum(device + N_REP, devices - 1)
        prev_rows = jnp.where(group > 0, feat_blocks[prev_dev, export_block[prev_dev, 0]], zero_block)
        next_rows = jnp.where(group < N_DOM - 1, feat_blocks[next_dev, export_block[next_dev, 0]], zero_block)
        beside = jnp.stack([prev_rows, next_rows])
        summed = jnp.dot(local_all[device].astype(jnp.bfloat16), feat_blocks[device].reshape(ROWS_DEV, F), preferred_element_type=jnp.float32).reshape(blocks, BLK, F)
        remote_part = jnp.einsum('qij,qjf->qif', remote_all[device].astype(jnp.float32), arrived.astype(jnp.float32))
        remote_hot = onehot(remote_dest[device])
        summed = summed + jnp.einsum('qb,qif->bif', remote_hot, remote_part, precision=highest)
        halo_part = jnp.einsum('qij,qjf->qif', halo_all[device].astype(jnp.float32), beside.astype(jnp.float32))
        halo_hot = onehot(halo_dest[device])
        summed = summed + jnp.einsum('qb,qif->bif', halo_hot, halo_part, precision=highest)
        degree = lax.optimization_barrier(jnp.sum(local_all[device], axis=1)).astype(jnp.float32)
        degree = degree + jnp.einsum('qb,qi->bi', remote_hot, lax.optimization_barrier(jnp.sum(remote_all[device], axis=2)).astype(jnp.float32), precision=highest).reshape(ROWS_DEV)
        degree = degree + jnp.einsum('qb,qi->bi', halo_hot, lax.optimization_barrier(jnp.sum(halo_all[device], axis=2)).astype(jnp.float32), precision=highest).reshape(ROWS_DEV)
        denom = jnp.maximum(degree, 1.0)
        return ((summed.reshape(ROWS_DEV, F) / denom[:, None]).astype(jnp.bfloat16), denom)
    neighbour_mean, denom = lax.map(forward_device, jnp.arange(devices, dtype=jnp.int32))
    neighbour_mean = neighbour_mean.reshape(NODES, F)
    denom = denom.reshape(NODES)
    linear = jnp.dot(features, w_self, preferred_element_type=jnp.float32) + jnp.dot(neighbour_mean, w_neigh, preferred_element_type=jnp.float32)
    output, pullback = jax.vjp(jax.nn.gelu, linear)
    linear_grad, = pullback(cotangent.astype(jnp.float32))
    linear_grad = linear_grad.astype(jnp.bfloat16)
    scale = 1.0 / jnp.sqrt(jnp.float32(NODES))
    self_grads = jnp.dot(features.T, linear_grad, preferred_element_type=jnp.float32) * scale
    neigh_grads = jnp.dot(neighbour_mean.T, linear_grad, preferred_element_type=jnp.float32) * scale
    mean_grad = (jnp.dot(linear_grad, w_neigh.T, preferred_element_type=jnp.float32) / denom[:, None]).astype(jnp.bfloat16)
    grad_blocks = mean_grad.reshape(devices, blocks, BLK, F)

    def halo_term(source_dev, side):
        counts = halo_all[source_dev, side].astype(jnp.float32)
        picked = grad_blocks[source_dev, halo_dest[source_dev, side]].astype(jnp.float32)
        return jnp.dot(counts.T, picked, precision=highest).astype(jnp.bfloat16)

    def backward_device(device):
        group = device // N_REP
        member_index = device % N_REP
        own = jnp.dot(local_all[device].astype(jnp.bfloat16).T, grad_blocks[device].reshape(ROWS_DEV, F), preferred_element_type=jnp.float32)
        receivers = group * N_REP + members
        counts = remote_all[receivers, member_index].astype(jnp.float32)
        picked = grad_blocks[receivers, remote_dest[receivers, member_index]].astype(jnp.float32)
        edge_terms = jnp.einsum('qij,qif->qjf', counts, picked).astype(jnp.bfloat16)
        total = own.reshape(blocks, BLK, F) + jnp.einsum('qb,qjf->bjf', onehot(send_block[device]), edge_terms.astype(jnp.float32), precision=highest)
        prev_dev = jnp.maximum(device - N_REP, 0)
        next_dev = jnp.minimum(device + N_REP, devices - 1)
        from_prev = jnp.where(group > 0, halo_term(prev_dev, 1), zero_block)
        from_next = jnp.where(group < N_DOM - 1, halo_term(next_dev, 0), zero_block)
        incoming = from_prev.astype(jnp.float32) + from_next.astype(jnp.float32)
        export_hot = onehot(export_block[device])[0]
        total = total + export_hot[:, None, None] * incoming[None, :, :]
        return total.reshape(ROWS_DEV, F)
    sparse_grads = lax.map(backward_device, jnp.arange(devices, dtype=jnp.int32)).reshape(NODES, F)
    feature_grads = (jnp.dot(linear_grad, w_self.T, preferred_element_type=jnp.float32) + sparse_grads).astype(jnp.bfloat16)
    return (output.astype(jnp.bfloat16), feature_grads, self_grads, neigh_grads)
```

```python
import functools
import math

import jax
import jax.numpy as jnp
from jax import lax
from jax.experimental import pallas as pl
from jax.experimental.pallas import tpu as pltpu
from jax.sharding import PartitionSpec as P

BLK = 128
MESH = pl.DeviceIdType.MESH
F32 = jnp.float32
BF16 = jnp.bfloat16


def dot(a, b):
    return jnp.dot(a, b, preferred_element_type=F32)


def dot_t(a, b):
    return lax.dot_general(a, b, (((0,), (0,)), ((), ())), preferred_element_type=F32)


def dot_nt(a, b):
    return lax.dot_general(a, b, (((1,), (1,)), ((), ())), preferred_element_type=F32)


def rows_at(start, size):
    return pl.ds(pl.multiple_of(start, size), size)


def kernel(
    domains, members, pieces, scale,
    feat_h, loc_h, rem_h, rdest_h, send_h, halo_h, hdest_h, exp_h, ws_h, wn_h, cot_h,
    out_h, fg_h, grads_h,
    pair, loc_v, rem_v, halo_v, ws_v, wn_v, cot_v, out_v, fg_v,
    rdest, send, hdest, export,
    outgoing, exported, arrived, beside, adj, acc, lin, lg, mg,
    mate_out, mate_in, own, xy_out, xy_in, zsum, z_out, z_in, grads,
    edge, returned, halo_edge, halo_back,
    in_sem, out_sem,
    f_send, f_recv, h_send, h_recv,
    m_send, m_recv, x_send, x_recv, z_send, z_recv,
    e_send, e_recv, b_send, b_recv,
    gz_send, gz_recv, gx_send, gx_recv, gm_send, gm_recv,
):
    dom = lax.axis_index("dom")
    me = lax.axis_index("rep")
    z = dom // 2
    core = dom % 2
    mate = dom + 1 - 2 * core
    zs = domains // 2
    rows, width = out_v.shape
    blocks = rows // BLK
    chunk = width // members
    piece = chunk // pieces
    peers = [(me + k) % members for k in range(1, members)]
    zpeers = [(z + k) % zs for k in range(1, zs)]
    has_prev = dom > 0
    has_next = dom < domains - 1
    sends = []

    def remote(src, dst, s_sem, r_sem, to):
        return pltpu.make_async_remote_copy(
            src_ref=src, dst_ref=dst, send_sem=s_sem, recv_sem=r_sem,
            device_id=to, device_id_type=MESH,
        )

    def push(*args):
        copy = remote(*args)
        copy.start()
        sends.append(copy)

    barrier = pltpu.get_barrier_semaphore()

    def greet(to):
        pl.semaphore_signal(barrier, inc=1, device_id=to, device_id_type=MESH)

    for q in peers:
        greet((dom, q))
    for j in zpeers:
        greet((j * 2 + core, me))
    greet((mate, me))
    outer = jnp.where(core == 0, dom - 1, dom + 1)
    has_outer = jnp.logical_and(outer >= 0, outer < domains)

    @pl.when(has_outer)
    def _():
        greet((outer, me))

    loads = {}
    for i, (name, src, dst) in enumerate([
        ("feat", feat_h, pair.at[0]), ("send", send_h, send), ("export", exp_h, export),
        ("rdest", rdest_h, rdest), ("hdest", hdest_h, hdest), ("loc", loc_h, loc_v),
        ("rem", rem_h, rem_v), ("halo", halo_h, halo_v), ("ws", ws_h, ws_v),
        ("wn", wn_h, wn_v), ("cot", cot_h, cot_v),
    ]):
        loads[name] = pltpu.make_async_copy(src, dst, in_sem.at[i])
        loads[name].start()

    for name in ("send", "export", "feat"):
        loads[name].wait()

    def picked(index):
        total = jnp.zeros((BLK, width), F32)
        for b in range(blocks):
            total = total + pair[0, b * BLK:(b + 1) * BLK, :].astype(F32) * (index == b).astype(F32)
        return total.astype(BF16)

    for q in peers:
        outgoing[rows_at(q * BLK, BLK), :] = picked(send[0, q])
    arrived[rows_at(me * BLK, BLK), :] = picked(send[0, me])
    exported[...] = picked(export[0, 0])

    pl.semaphore_wait(barrier, len(peers) + len(zpeers) + 1 + has_outer.astype(jnp.int32))

    for q in peers:
        push(
            outgoing.at[rows_at(q * BLK, BLK)], arrived.at[rows_at(me * BLK, BLK)],
            f_send.at[q], f_recv.at[me], (dom, q),
        )

    def exchange(sources, landing, s_sem, r_sem):
        to_prev = remote(sources[0], landing.at[pl.ds(BLK, BLK)], s_sem.at[0], r_sem.at[1], (dom - 1, me))
        to_next = remote(sources[1], landing.at[pl.ds(0, BLK)], s_sem.at[1], r_sem.at[0], (dom + 1, me))
        return to_prev, to_next

    def start_exchange(copies, landing):
        for slot, (there, copy) in enumerate(zip((has_prev, has_next), copies)):
            @pl.when(there)
            def _(copy=copy):
                copy.start()

            @pl.when(jnp.logical_not(there))
            def _(slot=slot):
                landing[pl.ds(slot * BLK, BLK), :] = jnp.zeros((BLK, width), BF16)

    def arrive_exchange(copies):
        to_prev, to_next = copies

        @pl.when(has_prev)
        def _():
            to_next.wait_recv()

        @pl.when(has_next)
        def _():
            to_prev.wait_recv()

    def end_exchange(copies):
        for there, copy in zip((has_prev, has_next), copies):
            @pl.when(there)
            def _(copy=copy):
                copy.wait_send()

    halo_f = exchange((exported, exported), beside, h_send, h_recv)
    start_exchange(halo_f, beside)

    for name in ("rdest", "hdest", "loc", "rem", "halo"):
        loads[name].wait()
    counts = loc_v[...].astype(F32)
    adj[:, :rows] = counts.astype(BF16)
    local_degree = jnp.sum(counts, axis=1, keepdims=True)
    for b in range(blocks):
        total = jnp.zeros((BLK, BLK), F32)
        for q in range(members + 2):
            if q < members:
                here = (rdest[0, q] == b).astype(F32)
                placed = rem_v[q].astype(F32) * here
            else:
                here = (hdest[0, q - members] == b).astype(F32)
                placed = halo_v[q - members].astype(F32) * here
            total = total + placed
            adj[b * BLK:(b + 1) * BLK, rows + q * BLK:rows + (q + 1) * BLK] = placed.astype(BF16)
        degree = jnp.sum(total, axis=1, keepdims=True) + local_degree[b * BLK:(b + 1) * BLK]
        acc[b * BLK:(b + 1) * BLK, :BLK] = jnp.broadcast_to(1.0 / jnp.maximum(degree, 1.0), (BLK, BLK))
    inverse = acc[:, :1]

    acc[...] = dot(adj[:, :rows], pair[0])
    loads["ws"].wait()
    lin[...] = dot(pair[0], ws_v[...])
    loads["wn"].wait()
    loads["cot"].wait()
    arrive_exchange(halo_f)
    acc[...] += dot(adj[:, rows + members * BLK:], beside[...])
    for q in peers:
        slot = arrived.at[rows_at(q * BLK, BLK)]
        remote(slot, slot, f_send.at[q], f_recv.at[q], (dom, q)).wait_recv()
    mean = (acc[...] + dot(adj[:, rows:rows + members * BLK], arrived[...])) * inverse
    pair[1] = mean.astype(BF16)

    x = lin[...] + dot(pair[1], wn_v[...])
    c = math.sqrt(2.0 / math.pi)
    square = x * x
    t = jnp.tanh(c * (x + 0.044715 * (x * square)))
    half = 0.5 * (1.0 + t)
    out_v[...] = (x * half).astype(BF16)
    slope = half + 0.5 * x * (1.0 - t * t) * (c * (1.0 + 3.0 * 0.044715 * square))
    lg[...] = (cot_v[...].astype(F32) * slope).astype(BF16)
    out_copy = pltpu.make_async_copy(out_v, out_h, out_sem.at[0])
    out_copy.start()

    mate_out[...] = dot_t(pair[1 - core], lg[...]).astype(BF16)
    order = peers + [me]
    for q in order:
        at = rows_at(q * chunk, chunk)
        push(mate_out.at[at], mate_in.at[at], m_send.at[q], m_recv.at[q], (mate, me))
    own[...] = dot_t(pair[core], lg[...])

    mg[...] = (dot_nt(lg[...], wn_v[...]) * inverse).astype(BF16)
    edge[...] = dot_t(adj[:, rows:rows + members * BLK], mg[...]).astype(BF16)
    halo_edge[...] = dot_t(adj[:, rows + members * BLK:], mg[...]).astype(BF16)
    returned[rows_at(me * BLK, BLK), :] = edge[rows_at(me * BLK, BLK), :]

    for q in order:
        at = rows_at(q * chunk, chunk)
        remote(mate_out.at[at], mate_in.at[at], m_send.at[q], m_recv.at[q], (mate, me)).wait_recv()
        both = own[at, :] + mate_in[at, :].astype(F32)
        if q is me:
            zsum[...] = both
        else:
            xy_out[at, :] = both.astype(BF16)
            push(xy_out.at[at], xy_in.at[rows_at(me * chunk, chunk)], x_send.at[q], x_recv.at[me], (dom, q))

    for q in peers:
        push(
            edge.at[rows_at(q * BLK, BLK)], returned.at[rows_at(me * BLK, BLK)],
            e_send.at[q], e_recv.at[me], (dom, q),
        )
    halo_b = exchange((halo_edge.at[pl.ds(0, BLK)], halo_edge.at[pl.ds(BLK, BLK)]), halo_back, b_send, b_recv)
    start_exchange(halo_b, halo_back)
    acc[...] = dot_nt(lg[...], ws_v[...]) + dot_t(adj[:, :rows], mg[...])

    for q in peers:
        at = rows_at(q * chunk, chunk)
        remote(xy_out.at[at], xy_in.at[at], x_send.at[q], x_recv.at[q], (dom, q)).wait_recv()
        zsum[...] += xy_in[at, :].astype(F32)

    def place(member, part):
        return rows_at((core * members + member) * chunk + part * piece, piece)

    def z_slot(j):
        return z_in.at[rows_at(j * piece, piece)]

    part = z if pieces > 1 else 0
    for j in zpeers:
        at = rows_at((j if pieces > 1 else 0) * piece, piece)
        to = rows_at(j * piece, piece)
        z_out[to, :] = zsum[at, :].astype(BF16)
        push(z_out.at[to], z_slot(z), z_send.at[j], z_recv.at[z], (j * 2 + core, me))
    z_in[rows_at(z * piece, piece), :] = zsum[rows_at(part * piece, piece), :].astype(BF16)
    for j in zpeers:
        remote(z_slot(j), z_slot(j), z_send.at[j], z_recv.at[j], (j * 2 + core, me)).wait_recv()
    total = z_in[:piece, :].astype(F32)
    for j in range(1, zs):
        total = total + z_in[j * piece:(j + 1) * piece, :].astype(F32)
    grads[place(me, part), :] = (total * scale).astype(BF16)

    def spread(part):
        at = grads.at[place(me, part)]
        for q in peers:
            push(at, at, gx_send.at[q * pieces + part], gx_recv.at[me * pieces + part], (dom, q))
        push(at, at, gm_send.at[me * pieces + part], gm_recv.at[me * pieces + part], (mate, me))

    if pieces > 1:
        at = grads.at[place(me, z)]
        for j in zpeers:
            push(at, at, gz_send.at[j], gz_recv.at[z], (j * 2 + core, me))
    spread(part)
    if pieces > 1:
        for j in zpeers:
            at = grads.at[place(me, j)]
            remote(at, at, gz_send.at[j], gz_recv.at[j], (j * 2 + core, me)).wait_recv()
            spread(j)

    arrive_exchange(halo_b)
    for q in peers:
        slot = returned.at[rows_at(q * BLK, BLK)]
        remote(slot, slot, e_send.at[q], e_recv.at[q], (dom, q)).wait_recv()
    incoming = halo_back[:BLK, :].astype(F32) + halo_back[BLK:, :].astype(F32)
    for b in range(blocks):
        total = acc[b * BLK:(b + 1) * BLK, :] + incoming * (export[0, 0] == b).astype(F32)
        for q in range(members):
            back = returned[q * BLK:(q + 1) * BLK, :].astype(F32)
            total = total + back * (send[0, q] == b).astype(F32)
        fg_v[b * BLK:(b + 1) * BLK, :] = total.astype(BF16)
    fg_copy = pltpu.make_async_copy(fg_v, fg_h, out_sem.at[1])
    fg_copy.start()

    parts = [part] + (zpeers if pieces > 1 else [])
    for j in parts:
        for q in peers:
            at = grads.at[place(q, j)]
            remote(at, at, gx_send.at[q * pieces + j], gx_recv.at[q * pieces + j], (dom, q)).wait_recv()
            push(at, at, gm_send.at[q * pieces + j], gm_recv.at[q * pieces + j], (mate, me))
    for j in parts:
        for q in order:
            at = grads.at[rows_at(((1 - core) * members + q) * chunk + j * piece, piece)]
            remote(at, at, gm_send.at[q * pieces + j], gm_recv.at[q * pieces + j], (mate, me)).wait_recv()
    grads_copy = pltpu.make_async_copy(grads, grads_h, out_sem.at[2])
    grads_copy.start()

    for copy in sends:
        copy.wait_send()
    end_exchange(halo_f)
    end_exchange(halo_b)
    out_copy.wait()
    fg_copy.wait()
    grads_copy.wait()


def body(domains, members, *args):
    features, w_self = args[0], args[8]
    rows, width = features.shape
    zs = domains // 2
    chunk = width // members
    pieces = zs if chunk % (16 * zs) == 0 else 1
    piece = chunk // pieces
    scale = 1.0 / math.sqrt(rows * members * domains)
    any_space = pl.BlockSpec(memory_space=pl.ANY)
    dma = pltpu.SemaphoreType.DMA

    def vmem(*shape, dtype=BF16):
        return pltpu.VMEM(shape, dtype)

    scratch = [
        vmem(2, rows, width),
        vmem(rows, rows, dtype=jnp.int32),
        vmem(members, BLK, BLK, dtype=jnp.int32),
        vmem(2, BLK, BLK, dtype=jnp.int32),
        vmem(width, width), vmem(width, width), vmem(rows, width),
        vmem(rows, width), vmem(rows, width),
        pltpu.SMEM((1, members), jnp.int32), pltpu.SMEM((1, members), jnp.int32),
        pltpu.SMEM((1, 2), jnp.int32), pltpu.SMEM((1, 1), jnp.int32),
        vmem(members * BLK, width), vmem(BLK, width), vmem(members * BLK, width), vmem(2 * BLK, width),
        vmem(rows, rows + (members + 2) * BLK),
        vmem(rows, width, dtype=F32), vmem(rows, width, dtype=F32),
        vmem(rows, width), vmem(rows, width),
        vmem(width, width), vmem(width, width), vmem(width, width, dtype=F32),
        vmem(width, width), vmem(width, width), vmem(chunk, width, dtype=F32),
        vmem(zs * piece, width), vmem(zs * piece, width), vmem(2 * width, width),
        vmem(members * BLK, width), vmem(members * BLK, width), vmem(2 * BLK, width), vmem(2 * BLK, width),
        dma((11,)), dma((3,)),
        dma((members,)), dma((members,)), dma((2,)), dma((2,)),
        dma((members,)), dma((members,)), dma((members,)), dma((members,)), dma((zs,)), dma((zs,)),
        dma((members,)), dma((members,)), dma((2,)), dma((2,)),
        dma((zs,)), dma((zs,)),
        dma((members * pieces,)), dma((members * pieces,)), dma((members * pieces,)), dma((members * pieces,)),
    ]
    output, feature_grads, grads = pl.pallas_call(
        functools.partial(kernel, domains, members, pieces, scale),
        out_shape=(
            jax.ShapeDtypeStruct((rows, width), BF16),
            jax.ShapeDtypeStruct((rows, width), BF16),
            jax.ShapeDtypeStruct((2 * width, width), BF16),
        ),
        in_specs=[any_space] * len(args),
        out_specs=(any_space,) * 3,
        scratch_shapes=scratch,
        compiler_params=pltpu.CompilerParams(
            collective_id=0, has_side_effects=True, vmem_limit_bytes=48 * 2**20
        ),
        name="sage_layer",
    )(*args)
    return output, feature_grads, grads[:width].astype(F32), grads[width:].astype(F32)


def solution(mesh):
    split = P(("dom", "rep"), None)
    split3 = P(("dom", "rep"), None, None)
    return jax.shard_map(
        functools.partial(body, mesh.shape["dom"], mesh.shape["rep"]),
        mesh=mesh,
        in_specs=(
            split, split, split3, split, split, split3, split, split, P(), P(), split,
        ),
        out_specs=(split, split, P(), P()),
        check_vma=False,
    )
```

```python
import functools
import math

import jax
import jax.numpy as jnp
from jax import lax
from jax.experimental import pallas as pl
from jax.experimental.pallas import tpu as pltpu
from jax.sharding import PartitionSpec as P

BLK = 128
MESH = pl.DeviceIdType.MESH
F32 = jnp.float32
BF16 = jnp.bfloat16


def dot(a, b):
    return jnp.dot(a, b, preferred_element_type=F32)


def dot_t(a, b):
    return lax.dot_general(a, b, (((0,), (0,)), ((), ())), preferred_element_type=F32)


def dot_nt(a, b):
    return lax.dot_general(a, b, (((1,), (1,)), ((), ())), preferred_element_type=F32)


def rows_at(start, size):
    return pl.ds(pl.multiple_of(start, size), size)


def kernel(
    domains, members, pieces, scale,
    feat_h, loc_h, rem_h, rdest_h, send_h, halo_h, hdest_h, exp_h, ws_h, wn_h, cot_h,
    out_h, fg_h, grads_h,
    pair, loc_v, rem_v, halo_v, ws_v, wn_v, cot_v, out_v, fg_v,
    rdest, send, hdest, export,
    outgoing, exported, arrived, beside, adj, acc, lin, lg, mg,
    mate_out, mate_in, own, xy_out, xy_in, z_out, z_in, grads,
    edge, returned, halo_edge, halo_back,
    in_sem, out_sem,
    f_send, f_recv, h_send, h_recv,
    m_send, m_recv, x_send, x_recv, z_send, z_recv,
    e_send, e_recv, b_send, b_recv,
    gz_send, gz_recv, gx_send, gx_recv, gm_send, gm_recv,
):
    dom = lax.axis_index("dom")
    me = lax.axis_index("rep")
    z = dom // 2
    core = dom % 2
    mate = dom + 1 - 2 * core
    zs = domains // 2
    rows, width = out_v.shape
    blocks = rows // BLK
    chunk = width // members
    piece = chunk // pieces
    peers = [(me + k) % members for k in range(1, members)]
    zpeers = [(z + k) % zs for k in range(1, zs)]
    has_prev = dom > 0
    has_next = dom < domains - 1
    sends = []

    def remote(src, dst, s_sem, r_sem, to):
        return pltpu.make_async_remote_copy(
            src_ref=src, dst_ref=dst, send_sem=s_sem, recv_sem=r_sem,
            device_id=to, device_id_type=MESH,
        )

    def push(*args):
        copy = remote(*args)
        copy.start()
        sends.append(copy)

    barrier = pltpu.get_barrier_semaphore()

    def greet(to):
        pl.semaphore_signal(barrier, inc=1, device_id=to, device_id_type=MESH)

    for q in peers:
        greet((dom, q))
    for j in zpeers:
        greet((j * 2 + core, me))
    greet((mate, me))
    outer = jnp.where(core == 0, dom - 1, dom + 1)
    has_outer = jnp.logical_and(outer >= 0, outer < domains)

    @pl.when(has_outer)
    def _():
        greet((outer, me))

    loads = {}
    for i, (name, src, dst) in enumerate([
        ("feat", feat_h, pair.at[0]), ("send", send_h, send), ("export", exp_h, export),
        ("rdest", rdest_h, rdest), ("hdest", hdest_h, hdest), ("loc", loc_h, loc_v),
        ("rem", rem_h, rem_v), ("halo", halo_h, halo_v), ("ws", ws_h, ws_v),
        ("wn", wn_h, wn_v), ("cot", cot_h, cot_v),
    ]):
        loads[name] = pltpu.make_async_copy(src, dst, in_sem.at[i])
        loads[name].start()

    for name in ("send", "export", "feat"):
        loads[name].wait()

    def picked(index):
        total = jnp.zeros((BLK, width), F32)
        for b in range(blocks):
            total = total + pair[0, b * BLK:(b + 1) * BLK, :].astype(F32) * (index == b).astype(F32)
        return total.astype(BF16)

    for q in peers:
        outgoing[rows_at(q * BLK, BLK), :] = picked(send[0, q])
    arrived[rows_at(me * BLK, BLK), :] = picked(send[0, me])
    exported[...] = picked(export[0, 0])

    pl.semaphore_wait(barrier, len(peers) + len(zpeers) + 1 + has_outer.astype(jnp.int32))

    for q in peers:
        push(
            outgoing.at[rows_at(q * BLK, BLK)], arrived.at[rows_at(me * BLK, BLK)],
            f_send.at[q], f_recv.at[me], (dom, q),
        )

    def exchange(sources, landing, s_sem, r_sem):
        to_prev = remote(sources[0], landing.at[pl.ds(BLK, BLK)], s_sem.at[0], r_sem.at[1], (dom - 1, me))
        to_next = remote(sources[1], landing.at[pl.ds(0, BLK)], s_sem.at[1], r_sem.at[0], (dom + 1, me))
        return to_prev, to_next

    def start_exchange(copies, landing):
        for slot, (there, copy) in enumerate(zip((has_prev, has_next), copies)):
            @pl.when(there)
            def _(copy=copy):
                copy.start()

            @pl.when(jnp.logical_not(there))
            def _(slot=slot):
                landing[pl.ds(slot * BLK, BLK), :] = jnp.zeros((BLK, width), BF16)

    def arrive_exchange(copies):
        to_prev, to_next = copies

        @pl.when(has_prev)
        def _():
            to_next.wait_recv()

        @pl.when(has_next)
        def _():
            to_prev.wait_recv()

    def end_exchange(copies):
        for there, copy in zip((has_prev, has_next), copies):
            @pl.when(there)
            def _(copy=copy):
                copy.wait_send()

    halo_f = exchange((exported, exported), beside, h_send, h_recv)
    start_exchange(halo_f, beside)

    for name in ("rdest", "hdest", "loc", "rem", "halo"):
        loads[name].wait()
    counts = loc_v[...].astype(F32)
    adj[:, :rows] = counts.astype(BF16)
    local_degree = jnp.sum(counts, axis=1, keepdims=True)
    for b in range(blocks):
        total = jnp.zeros((BLK, BLK), F32)
        for q in range(members + 2):
            if q < members:
                here = (rdest[0, q] == b).astype(F32)
                placed = rem_v[q].astype(F32) * here
            else:
                here = (hdest[0, q - members] == b).astype(F32)
                placed = halo_v[q - members].astype(F32) * here
            total = total + placed
            adj[b * BLK:(b + 1) * BLK, rows + q * BLK:rows + (q + 1) * BLK] = placed.astype(BF16)
        degree = jnp.sum(total, axis=1, keepdims=True) + local_degree[b * BLK:(b + 1) * BLK]
        acc[b * BLK:(b + 1) * BLK, :BLK] = jnp.broadcast_to(1.0 / jnp.maximum(degree, 1.0), (BLK, BLK))
    inverse = acc[:, :1]

    acc[...] = dot(adj[:, :rows], pair[0])
    loads["ws"].wait()
    lin[...] = dot(pair[0], ws_v[...])
    loads["wn"].wait()
    loads["cot"].wait()
    arrive_exchange(halo_f)
    acc[...] += dot(adj[:, rows + members * BLK:], beside[...])
    for q in peers:
        slot = arrived.at[rows_at(q * BLK, BLK)]
        remote(slot, slot, f_send.at[q], f_recv.at[q], (dom, q)).wait_recv()
    mean = (acc[...] + dot(adj[:, rows:rows + members * BLK], arrived[...])) * inverse
    pair[1] = mean.astype(BF16)

    x = lin[...] + dot(pair[1], wn_v[...])
    c = math.sqrt(2.0 / math.pi)
    square = x * x
    t = jnp.tanh(c * (x + 0.044715 * (x * square)))
    half = 0.5 * (1.0 + t)
    out_v[...] = (x * half).astype(BF16)
    slope = half + 0.5 * x * (1.0 - t * t) * (c * (1.0 + 3.0 * 0.044715 * square))
    lg[...] = (cot_v[...].astype(F32) * slope).astype(BF16)
    out_copy = pltpu.make_async_copy(out_v, out_h, out_sem.at[0])
    out_copy.start()

    layer = members * piece
    parts = [(z + k) % zs for k in range(1, zs)] + [z] if pieces > 1 else [0]
    mine = parts[-1]
    mate_out[...] = dot_t(pair[1 - core], lg[...]).astype(BF16)

    def mate_copy(j):
        at = rows_at(j * layer, layer)
        return mate_out.at[at], mate_in.at[at], m_send.at[j], m_recv.at[j], (mate, me)

    for j in parts:
        push(*mate_copy(j))
    own[...] = dot_t(pair[core], lg[...])
    for n, j in enumerate(parts):
        remote(*mate_copy(j)).wait_recv()
        at = rows_at(j * layer, layer)
        own[at, :] += mate_in[at, :].astype(F32)
        xy_out[at, :] = own[at, :].astype(BF16)
        for q in peers:
            push(
                xy_out.at[rows_at(j * layer + q * piece, piece)],
                xy_in.at[rows_at((me * pieces + j) * piece, piece)],
                x_send.at[q * pieces + j], x_recv.at[me * pieces + j], (dom, q),
            )

    mg[...] = (dot_nt(lg[...], wn_v[...]) * inverse).astype(BF16)
    edge[...] = dot_t(adj[:, rows:rows + members * BLK], mg[...]).astype(BF16)
    halo_edge[...] = dot_t(adj[:, rows + members * BLK:], mg[...]).astype(BF16)
    returned[rows_at(me * BLK, BLK), :] = edge[rows_at(me * BLK, BLK), :]
    for q in peers:
        push(
            edge.at[rows_at(q * BLK, BLK)], returned.at[rows_at(me * BLK, BLK)],
            e_send.at[q], e_recv.at[me], (dom, q),
        )
    halo_b = exchange((halo_edge.at[pl.ds(0, BLK)], halo_edge.at[pl.ds(BLK, BLK)]), halo_back, b_send, b_recv)
    start_exchange(halo_b, halo_back)

    def z_slot(j):
        return z_in.at[rows_at(j * piece, piece)]

    for j in parts:
        total = own[rows_at(j * layer + me * piece, piece), :]
        for q in peers:
            slot = rows_at((q * pieces + j) * piece, piece)
            remote(
                xy_in.at[slot], xy_in.at[slot],
                x_send.at[q * pieces + j], x_recv.at[q * pieces + j], (dom, q),
            ).wait_recv()
            total = total + xy_in[slot, :].astype(F32)
        total = total.astype(BF16)
        targets = [j] if pieces > 1 else zpeers
        if pieces == 1 or j is not mine:
            for to in targets:
                out = rows_at(to * piece, piece)
                z_out[out, :] = total
                push(z_out.at[out], z_slot(z), z_send.at[to], z_recv.at[z], (to * 2 + core, me))
        if j is mine:
            z_in[rows_at(z * piece, piece), :] = total
    acc[...] = dot_nt(lg[...], ws_v[...]) + dot_t(adj[:, :rows], mg[...])
    for j in zpeers:
        remote(z_slot(j), z_slot(j), z_send.at[j], z_recv.at[j], (j * 2 + core, me)).wait_recv()
    total = z_in[:piece, :].astype(F32)
    for j in range(1, zs):
        total = total + z_in[j * piece:(j + 1) * piece, :].astype(F32)

    def place(member, part, half=core):
        return rows_at(half * width + part * layer + member * piece, piece)

    grads[place(me, mine), :] = (total * scale).astype(BF16)

    def to_mate(member, j):
        at = grads.at[place(member, j)]
        push(at, at, gm_send.at[member * pieces + j], gm_recv.at[member * pieces + j], (mate, me))

    def to_peer(q, member, j):
        at = grads.at[place(member, j)]
        push(at, at, gx_send.at[q * pieces + j], gx_recv.at[member * pieces + j], (dom, q))

    def from_peer(member, j):
        at = grads.at[place(member, j)]
        remote(at, at, gx_send.at[member * pieces + j], gx_recv.at[member * pieces + j], (dom, member)).wait_recv()

    relay = members == 4
    beside_x = me + 1 - 2 * (me % 2)
    beside_y = (me + 2) % 4
    direct = [beside_x, beside_y] if relay else peers

    def spread(j):
        for q in direct:
            to_peer(q, me, j)
        to_mate(me, j)

    if pieces > 1:
        at = grads.at[place(me, z)]
        for j in zpeers:
            push(at, at, gz_send.at[j], gz_recv.at[z], (j * 2 + core, me))
    spread(mine)
    if pieces > 1:
        for j in zpeers:
            at = grads.at[place(me, j)]
            remote(at, at, gz_send.at[j], gz_recv.at[j], (j * 2 + core, me)).wait_recv()
            spread(j)

    arrivals = [mine] + (zpeers if pieces > 1 else [])
    for j in arrivals:
        for q in direct:
            from_peer(q, j)
        if relay:
            first = j % 2
            source = beside_x * (1 - first) + beside_y * first
            to_peer(beside_x + beside_y - source, source, j)
        for q in direct:
            to_mate(q, j)

    arrive_exchange(halo_b)
    for q in peers:
        slot = returned.at[rows_at(q * BLK, BLK)]
        remote(slot, slot, e_send.at[q], e_recv.at[q], (dom, q)).wait_recv()
    incoming = halo_back[:BLK, :].astype(F32) + halo_back[BLK:, :].astype(F32)
    for b in range(blocks):
        total = acc[b * BLK:(b + 1) * BLK, :] + incoming * (export[0, 0] == b).astype(F32)
        for q in range(members):
            back = returned[q * BLK:(q + 1) * BLK, :].astype(F32)
            total = total + back * (send[0, q] == b).astype(F32)
        fg_v[b * BLK:(b + 1) * BLK, :] = total.astype(BF16)
    fg_copy = pltpu.make_async_copy(fg_v, fg_h, out_sem.at[1])
    fg_copy.start()

    if relay:
        across = (beside_x + 2) % 4
        for j in arrivals:
            from_peer(across, j)
            to_mate(across, j)
    for j in arrivals:
        for q in [me] + peers:
            at = grads.at[place(q, j, 1 - core)]
            remote(at, at, gm_send.at[q * pieces + j], gm_recv.at[q * pieces + j], (mate, me)).wait_recv()
    grads_copy = pltpu.make_async_copy(grads, grads_h, out_sem.at[2])
    grads_copy.start()

    for copy in sends:
        copy.wait_send()
    end_exchange(halo_f)
    end_exchange(halo_b)
    out_copy.wait()
    fg_copy.wait()
    grads_copy.wait()


def finish(out_i, fg_i, grads_i, out_o, fg_o, self_o, neigh_o, narrow, wide, load_sem, sem):
    width = self_o.shape[0]
    loads = []
    for start in range(0, 2 * width, BLK):
        at = pl.ds(start, BLK)
        loads.append(pltpu.make_async_copy(grads_i.at[at], narrow.at[at], load_sem.at[start // BLK]))
        loads[-1].start()
    copies = [
        pltpu.make_async_copy(out_i, out_o, sem.at[0]),
        pltpu.make_async_copy(fg_i, fg_o, sem.at[1]),
    ]
    for copy in copies:
        copy.start()
    for start in range(0, 2 * width, BLK):
        at = pl.ds(start, BLK)
        loads[start // BLK].wait()
        wide[at, :] = narrow[at, :].astype(F32)
        dst = self_o if start < width else neigh_o
        copy = pltpu.make_async_copy(
            wide.at[at], dst.at[pl.ds(start % width, BLK)], sem.at[2 + start // BLK]
        )
        copy.start()
        copies.append(copy)
    for copy in copies:
        copy.wait()


def body(domains, members, *args):
    features, w_self = args[0], args[8]
    rows, width = features.shape
    zs = domains // 2
    chunk = width // members
    pieces = zs if chunk % (16 * zs) == 0 else 1
    piece = chunk // pieces
    scale = 1.0 / math.sqrt(rows * members * domains)
    any_space = pl.BlockSpec(memory_space=pl.ANY)
    dma = pltpu.SemaphoreType.DMA

    def vmem(*shape, dtype=BF16):
        return pltpu.VMEM(shape, dtype)

    scratch = [
        vmem(2, rows, width),
        vmem(rows, rows, dtype=jnp.int32),
        vmem(members, BLK, BLK, dtype=jnp.int32),
        vmem(2, BLK, BLK, dtype=jnp.int32),
        vmem(width, width), vmem(width, width), vmem(rows, width),
        vmem(rows, width), vmem(rows, width),
        pltpu.SMEM((1, members), jnp.int32), pltpu.SMEM((1, members), jnp.int32),
        pltpu.SMEM((1, 2), jnp.int32), pltpu.SMEM((1, 1), jnp.int32),
        vmem(members * BLK, width), vmem(BLK, width), vmem(members * BLK, width), vmem(2 * BLK, width),
        vmem(rows, rows + (members + 2) * BLK),
        vmem(rows, width, dtype=F32), vmem(rows, width, dtype=F32),
        vmem(rows, width), vmem(rows, width),
        vmem(width, width), vmem(width, width), vmem(width, width, dtype=F32),
        vmem(width, width), vmem(width, width),
        vmem(zs * piece, width), vmem(zs * piece, width), vmem(2 * width, width),
        vmem(members * BLK, width), vmem(members * BLK, width), vmem(2 * BLK, width), vmem(2 * BLK, width),
        dma((11,)), dma((3,)),
        dma((members,)), dma((members,)), dma((2,)), dma((2,)),
        dma((pieces,)), dma((pieces,)), dma((members * pieces,)), dma((members * pieces,)), dma((zs,)), dma((zs,)),
        dma((members,)), dma((members,)), dma((2,)), dma((2,)),
        dma((zs,)), dma((zs,)),
        dma((members * pieces,)), dma((members * pieces,)), dma((members * pieces,)), dma((members * pieces,)),
    ]
    output, feature_grads, grads = pl.pallas_call(
        functools.partial(kernel, domains, members, pieces, scale),
        out_shape=(
            jax.ShapeDtypeStruct((rows, width), BF16),
            jax.ShapeDtypeStruct((rows, width), BF16),
            jax.ShapeDtypeStruct((2 * width, width), BF16),
        ),
        in_specs=[any_space] * len(args),
        out_specs=(any_space,) * 3,
        scratch_shapes=scratch,
        compiler_params=pltpu.CompilerParams(
            collective_id=0, has_side_effects=True, vmem_limit_bytes=60 * 2**20
        ),
        name="sage_layer",
    )(*args)
    return pl.pallas_call(
        finish,
        out_shape=(
            jax.ShapeDtypeStruct((rows, width), BF16),
            jax.ShapeDtypeStruct((rows, width), BF16),
            jax.ShapeDtypeStruct((width, width), F32),
            jax.ShapeDtypeStruct((width, width), F32),
        ),
        in_specs=[any_space] * 3,
        out_specs=(any_space,) * 4,
        scratch_shapes=[
            vmem(2 * width, width), vmem(2 * width, width, dtype=F32),
            dma((2 * width // BLK,)), dma((2 + 2 * width // BLK,)),
        ],
        compiler_params=pltpu.CompilerParams(vmem_limit_bytes=60 * 2**20),
        name="finish",
    )(output, feature_grads, grads)


def solution(mesh):
    split = P(("dom", "rep"), None)
    split3 = P(("dom", "rep"), None, None)
    return jax.shard_map(
        functools.partial(body, mesh.shape["dom"], mesh.shape["rep"]),
        mesh=mesh,
        in_specs=(
            split, split, split3, split, split, split3, split, split, P(), P(), split,
        ),
        out_specs=(split, split, P(), P()),
        check_vma=False,
    )
```

```python
import functools
import math

import jax
import jax.numpy as jnp
from jax import lax
from jax.experimental import pallas as pl
from jax.experimental.pallas import tpu as pltpu
from jax.sharding import PartitionSpec as P

BLK = 128
MESH = pl.DeviceIdType.MESH
F32 = jnp.float32
BF16 = jnp.bfloat16


def dot(a, b):
    return jnp.dot(a, b, preferred_element_type=F32)


def dot_t(a, b):
    return lax.dot_general(a, b, (((0,), (0,)), ((), ())), preferred_element_type=F32)


def dot_nt(a, b):
    return lax.dot_general(a, b, (((1,), (1,)), ((), ())), preferred_element_type=F32)


def rows_at(start, size):
    return pl.ds(pl.multiple_of(start, size), size)


def kernel(
    domains, members, pieces, scale,
    feat_h, loc_h, rem_h, rdest_h, send_h, halo_h, hdest_h, exp_h, ws_h, wn_h, cot_h,
    out_h, fg_h, grads_h,
    pair, loc_v, rem_v, halo_v, ws_v, wn_v, cot_v, out_v, fg_v,
    rdest, send, hdest, export,
    outgoing, exported, arrived, beside, adj, acc, lin, lg, mg,
    mate_out, mate_in, own, xy_out, xy_in, z_out, z_in, grads,
    edge, returned, halo_edge, halo_back,
    in_sem, out_sem,
    f_send, f_recv, h_send, h_recv,
    m_send, m_recv, x_send, x_recv, z_send, z_recv,
    e_send, e_recv, b_send, b_recv,
    gz_send, gz_recv, gx_send, gx_recv, gm_send, gm_recv,
):
    dom = lax.axis_index("dom")
    me = lax.axis_index("rep")
    z = dom // 2
    core = dom % 2
    mate = dom + 1 - 2 * core
    zs = domains // 2
    rows, width = out_v.shape
    blocks = rows // BLK
    chunk = width // members
    piece = chunk // pieces
    relay = members == 4
    beside_x = me + 1 - 2 * (me % 2)
    beside_y = (me + 2) % 4
    across = 3 - me
    peers = [across, beside_x, beside_y] if relay else [(me + k) % members for k in range(1, members)]
    zpeers = [(z + k) % zs for k in range(1, zs)]
    has_prev = dom > 0
    has_next = dom < domains - 1
    sends = []

    def remote(src, dst, s_sem, r_sem, to):
        return pltpu.make_async_remote_copy(
            src_ref=src, dst_ref=dst, send_sem=s_sem, recv_sem=r_sem,
            device_id=to, device_id_type=MESH,
        )

    def push(*args):
        copy = remote(*args)
        copy.start()
        sends.append(copy)

    barrier = pltpu.get_barrier_semaphore()

    def greet(to):
        pl.semaphore_signal(barrier, inc=1, device_id=to, device_id_type=MESH)

    for q in peers:
        greet((dom, q))
    for j in zpeers:
        greet((j * 2 + core, me))
    greet((mate, me))
    outer = jnp.where(core == 0, dom - 1, dom + 1)
    has_outer = jnp.logical_and(outer >= 0, outer < domains)

    @pl.when(has_outer)
    def _():
        greet((outer, me))

    loads = {}
    for i, (name, src, dst) in enumerate([
        ("feat", feat_h, pair.at[0]), ("send", send_h, send), ("export", exp_h, export),
        ("rdest", rdest_h, rdest), ("hdest", hdest_h, hdest), ("loc", loc_h, loc_v),
        ("rem", rem_h, rem_v), ("halo", halo_h, halo_v), ("ws", ws_h, ws_v),
        ("wn", wn_h, wn_v), ("cot", cot_h, cot_v),
    ]):
        loads[name] = pltpu.make_async_copy(src, dst, in_sem.at[i])
        loads[name].start()

    for name in ("send", "export", "feat"):
        loads[name].wait()

    def picked(index):
        total = jnp.zeros((BLK, width), F32)
        for b in range(blocks):
            total = total + pair[0, b * BLK:(b + 1) * BLK, :].astype(F32) * (index == b).astype(F32)
        return total.astype(BF16)

    for q in peers:
        outgoing[rows_at(q * BLK, BLK), :] = picked(send[0, q])
    arrived[rows_at(me * BLK, BLK), :] = picked(send[0, me])
    exported[...] = picked(export[0, 0])

    pl.semaphore_wait(barrier, len(peers) + len(zpeers) + 1 + has_outer.astype(jnp.int32))

    for q in peers:
        push(
            outgoing.at[rows_at(q * BLK, BLK)], arrived.at[rows_at(me * BLK, BLK)],
            f_send.at[q], f_recv.at[me], (dom, q),
        )

    def exchange(sources, landing, s_sem, r_sem):
        to_prev = remote(sources[0], landing.at[pl.ds(BLK, BLK)], s_sem.at[0], r_sem.at[1], (dom - 1, me))
        to_next = remote(sources[1], landing.at[pl.ds(0, BLK)], s_sem.at[1], r_sem.at[0], (dom + 1, me))
        return to_prev, to_next

    def start_exchange(copies, landing):
        for slot, (there, copy) in enumerate(zip((has_prev, has_next), copies)):
            @pl.when(there)
            def _(copy=copy):
                copy.start()

            @pl.when(jnp.logical_not(there))
            def _(slot=slot):
                landing[pl.ds(slot * BLK, BLK), :] = jnp.zeros((BLK, width), BF16)

    def arrive_exchange(copies):
        to_prev, to_next = copies

        @pl.when(has_prev)
        def _():
            to_next.wait_recv()

        @pl.when(has_next)
        def _():
            to_prev.wait_recv()

    def end_exchange(copies):
        for there, copy in zip((has_prev, has_next), copies):
            @pl.when(there)
            def _(copy=copy):
                copy.wait_send()

    halo_f = exchange((exported, exported), beside, h_send, h_recv)
    start_exchange(halo_f, beside)

    for name in ("rdest", "hdest", "loc", "rem", "halo"):
        loads[name].wait()
    counts = loc_v[...].astype(F32)
    adj[:, :rows] = counts.astype(BF16)
    local_degree = jnp.sum(counts, axis=1, keepdims=True)
    for b in range(blocks):
        total = jnp.zeros((BLK, BLK), F32)
        for q in range(members + 2):
            if q < members:
                here = (rdest[0, q] == b).astype(F32)
                placed = rem_v[q].astype(F32) * here
            else:
                here = (hdest[0, q - members] == b).astype(F32)
                placed = halo_v[q - members].astype(F32) * here
            total = total + placed
            adj[b * BLK:(b + 1) * BLK, rows + q * BLK:rows + (q + 1) * BLK] = placed.astype(BF16)
        degree = jnp.sum(total, axis=1, keepdims=True) + local_degree[b * BLK:(b + 1) * BLK]
        acc[b * BLK:(b + 1) * BLK, :BLK] = jnp.broadcast_to(1.0 / jnp.maximum(degree, 1.0), (BLK, BLK))
    inverse = acc[:, :1]

    acc[...] = dot(adj[:, :rows], pair[0])
    loads["ws"].wait()
    lin[...] = dot(pair[0], ws_v[...])
    loads["wn"].wait()
    loads["cot"].wait()
    arrive_exchange(halo_f)
    acc[...] += dot(adj[:, rows + members * BLK:], beside[...])
    for q in peers:
        slot = arrived.at[rows_at(q * BLK, BLK)]
        remote(slot, slot, f_send.at[q], f_recv.at[q], (dom, q)).wait_recv()
    mean = (acc[...] + dot(adj[:, rows:rows + members * BLK], arrived[...])) * inverse
    pair[1] = mean.astype(BF16)

    x = lin[...] + dot(pair[1], wn_v[...])
    c = math.sqrt(2.0 / math.pi)
    square = x * x
    t = jnp.tanh(c * (x + 0.044715 * (x * square)))
    half = 0.5 * (1.0 + t)
    out_v[...] = (x * half).astype(BF16)
    slope = half + 0.5 * x * (1.0 - t * t) * (c * (1.0 + 3.0 * 0.044715 * square))
    lg[...] = (cot_v[...].astype(F32) * slope).astype(BF16)
    out_copy = pltpu.make_async_copy(out_v, out_h, out_sem.at[0])
    out_copy.start()

    layer = members * piece
    parts = [(z + k) % zs for k in range(1, zs)] + [z] if pieces > 1 else [0]
    mine = parts[-1]
    mate_out[...] = dot_t(pair[1 - core], lg[...]).astype(BF16)

    def mate_copy(j):
        at = rows_at(j * layer, layer)
        return mate_out.at[at], mate_in.at[at], m_send.at[j], m_recv.at[j], (mate, me)

    for j in parts:
        push(*mate_copy(j))
    own[...] = dot_t(pair[core], lg[...])
    for n, j in enumerate(parts):
        remote(*mate_copy(j)).wait_recv()
        at = rows_at(j * layer, layer)
        own[at, :] += mate_in[at, :].astype(F32)
        xy_out[at, :] = own[at, :].astype(BF16)
        for q in peers:
            push(
                xy_out.at[rows_at(j * layer + q * piece, piece)],
                xy_in.at[rows_at((me * pieces + j) * piece, piece)],
                x_send.at[q * pieces + j], x_recv.at[me * pieces + j], (dom, q),
            )

    mg[...] = (dot_nt(lg[...], wn_v[...]) * inverse).astype(BF16)
    edge[...] = dot_t(adj[:, rows:rows + members * BLK], mg[...]).astype(BF16)
    halo_edge[...] = dot_t(adj[:, rows + members * BLK:], mg[...]).astype(BF16)
    returned[rows_at(me * BLK, BLK), :] = edge[rows_at(me * BLK, BLK), :]
    halo_b = exchange((halo_edge.at[pl.ds(0, BLK)], halo_edge.at[pl.ds(BLK, BLK)]), halo_back, b_send, b_recv)
    start_exchange(halo_b, halo_back)

    def z_slot(j):
        return z_in.at[rows_at(j * piece, piece)]

    for j in parts:
        total = own[rows_at(j * layer + me * piece, piece), :]
        for q in peers:
            slot = rows_at((q * pieces + j) * piece, piece)
            remote(
                xy_in.at[slot], xy_in.at[slot],
                x_send.at[q * pieces + j], x_recv.at[q * pieces + j], (dom, q),
            ).wait_recv()
            total = total + xy_in[slot, :].astype(F32)
        total = total.astype(BF16)
        targets = [j] if pieces > 1 else zpeers
        if pieces == 1 or j is not mine:
            for to in targets:
                out = rows_at(to * piece, piece)
                z_out[out, :] = total
                push(z_out.at[out], z_slot(z), z_send.at[to], z_recv.at[z], (to * 2 + core, me))
        if j is mine:
            z_in[rows_at(z * piece, piece), :] = total
    for q in peers:
        push(
            edge.at[rows_at(q * BLK, BLK)], returned.at[rows_at(me * BLK, BLK)],
            e_send.at[q], e_recv.at[me], (dom, q),
        )
    acc[...] = dot_nt(lg[...], ws_v[...]) + dot_t(adj[:, :rows], mg[...])
    for j in zpeers:
        remote(z_slot(j), z_slot(j), z_send.at[j], z_recv.at[j], (j * 2 + core, me)).wait_recv()
    total = z_in[:piece, :].astype(F32)
    for j in range(1, zs):
        total = total + z_in[j * piece:(j + 1) * piece, :].astype(F32)

    def place(member, part, half=core):
        return rows_at(half * width + part * layer + member * piece, piece)

    grads[place(me, mine), :] = (total * scale).astype(BF16)

    def to_mate(member, j):
        at = grads.at[place(member, j)]
        push(at, at, gm_send.at[member * pieces + j], gm_recv.at[member * pieces + j], (mate, me))

    def to_peer(q, member, j):
        at = grads.at[place(member, j)]
        push(at, at, gx_send.at[q * pieces + j], gx_recv.at[member * pieces + j], (dom, q))

    def from_peer(member, j):
        at = grads.at[place(member, j)]
        remote(at, at, gx_send.at[member * pieces + j], gx_recv.at[member * pieces + j], (dom, member)).wait_recv()

    direct = [beside_x, beside_y] if relay else peers

    def spread(j):
        for q in direct:
            to_peer(q, me, j)
        to_mate(me, j)

    if pieces > 1:
        at = grads.at[place(me, z)]
        for j in zpeers:
            push(at, at, gz_send.at[j], gz_recv.at[z], (j * 2 + core, me))
    spread(mine)
    if pieces > 1:
        for j in zpeers:
            at = grads.at[place(me, j)]
            remote(at, at, gz_send.at[j], gz_recv.at[j], (j * 2 + core, me)).wait_recv()
            spread(j)

    arrivals = [mine] + (zpeers if pieces > 1 else [])
    for j in arrivals:
        for q in direct:
            from_peer(q, j)
        if relay:
            first = j % 2
            source = beside_x * (1 - first) + beside_y * first
            to_peer(beside_x + beside_y - source, source, j)
        for q in direct:
            to_mate(q, j)

    arrive_exchange(halo_b)
    for q in peers:
        slot = returned.at[rows_at(q * BLK, BLK)]
        remote(slot, slot, e_send.at[q], e_recv.at[q], (dom, q)).wait_recv()
    incoming = halo_back[:BLK, :].astype(F32) + halo_back[BLK:, :].astype(F32)
    for b in range(blocks):
        total = acc[b * BLK:(b + 1) * BLK, :] + incoming * (export[0, 0] == b).astype(F32)
        for q in range(members):
            back = returned[q * BLK:(q + 1) * BLK, :].astype(F32)
            total = total + back * (send[0, q] == b).astype(F32)
        fg_v[b * BLK:(b + 1) * BLK, :] = total.astype(BF16)
    fg_copy = pltpu.make_async_copy(fg_v, fg_h, out_sem.at[1])
    fg_copy.start()

    if relay:
        for j in arrivals:
            from_peer(across, j)
            to_mate(across, j)
    writes = []

    def write(half, j):
        at = rows_at(half * width + j * layer, layer)
        copy = pltpu.make_async_copy(grads.at[at], grads_h.at[at], out_sem.at[2 + len(writes)])
        copy.start()
        writes.append(copy)

    for j in arrivals:
        write(core, j)
    for j in arrivals:
        for q in [me] + peers:
            at = grads.at[place(q, j, 1 - core)]
            remote(at, at, gm_send.at[q * pieces + j], gm_recv.at[q * pieces + j], (mate, me)).wait_recv()
        write(1 - core, j)

    for copy in sends:
        copy.wait_send()
    end_exchange(halo_f)
    end_exchange(halo_b)
    out_copy.wait()
    fg_copy.wait()
    for copy in writes:
        copy.wait()


def finish(out_i, fg_i, grads_i, out_o, fg_o, self_o, neigh_o, out_v, fg_v, narrow, wide, load_sem, sem):
    width = self_o.shape[0]
    starts = range(0, 2 * width, BLK)
    loads = [
        pltpu.make_async_copy(grads_i.at[pl.ds(start, BLK)], narrow.at[pl.ds(start, BLK)], load_sem.at[2 + n])
        for n, start in enumerate(starts)
    ]
    loads += [
        pltpu.make_async_copy(out_i, out_v, load_sem.at[0]),
        pltpu.make_async_copy(fg_i, fg_v, load_sem.at[1]),
    ]
    for copy in loads:
        copy.start()
    stores = []
    for n, start in enumerate(starts):
        at = pl.ds(start, BLK)
        loads[n].wait()
        wide[at, :] = narrow[at, :].astype(F32)
        dst = self_o if start < width else neigh_o
        stores.append(pltpu.make_async_copy(wide.at[at], dst.at[pl.ds(start % width, BLK)], sem.at[2 + n]))
        stores[-1].start()
    for n, (src, dst) in enumerate(((out_v, out_o), (fg_v, fg_o))):
        loads[n - 2].wait()
        stores.append(pltpu.make_async_copy(src, dst, sem.at[n]))
        stores[-1].start()
    for copy in stores:
        copy.wait()


def body(domains, members, *args):
    features, w_self = args[0], args[8]
    rows, width = features.shape
    zs = domains // 2
    chunk = width // members
    pieces = zs if chunk % (16 * zs) == 0 else 1
    piece = chunk // pieces
    scale = 1.0 / math.sqrt(rows * members * domains)
    any_space = pl.BlockSpec(memory_space=pl.ANY)
    dma = pltpu.SemaphoreType.DMA

    def vmem(*shape, dtype=BF16):
        return pltpu.VMEM(shape, dtype)

    scratch = [
        vmem(2, rows, width),
        vmem(rows, rows, dtype=jnp.int32),
        vmem(members, BLK, BLK, dtype=jnp.int32),
        vmem(2, BLK, BLK, dtype=jnp.int32),
        vmem(width, width), vmem(width, width), vmem(rows, width),
        vmem(rows, width), vmem(rows, width),
        pltpu.SMEM((1, members), jnp.int32), pltpu.SMEM((1, members), jnp.int32),
        pltpu.SMEM((1, 2), jnp.int32), pltpu.SMEM((1, 1), jnp.int32),
        vmem(members * BLK, width), vmem(BLK, width), vmem(members * BLK, width), vmem(2 * BLK, width),
        vmem(rows, rows + (members + 2) * BLK),
        vmem(rows, width, dtype=F32), vmem(rows, width, dtype=F32),
        vmem(rows, width), vmem(rows, width),
        vmem(width, width), vmem(width, width), vmem(width, width, dtype=F32),
        vmem(width, width), vmem(width, width),
        vmem(zs * piece, width), vmem(zs * piece, width), vmem(2 * width, width),
        vmem(members * BLK, width), vmem(members * BLK, width), vmem(2 * BLK, width), vmem(2 * BLK, width),
        dma((11,)), dma((2 + 2 * pieces,)),
        dma((members,)), dma((members,)), dma((2,)), dma((2,)),
        dma((pieces,)), dma((pieces,)), dma((members * pieces,)), dma((members * pieces,)), dma((zs,)), dma((zs,)),
        dma((members,)), dma((members,)), dma((2,)), dma((2,)),
        dma((zs,)), dma((zs,)),
        dma((members * pieces,)), dma((members * pieces,)), dma((members * pieces,)), dma((members * pieces,)),
    ]
    output, feature_grads, grads = pl.pallas_call(
        functools.partial(kernel, domains, members, pieces, scale),
        out_shape=(
            jax.ShapeDtypeStruct((rows, width), BF16),
            jax.ShapeDtypeStruct((rows, width), BF16),
            jax.ShapeDtypeStruct((2 * width, width), BF16),
        ),
        in_specs=[any_space] * len(args),
        out_specs=(any_space,) * 3,
        scratch_shapes=scratch,
        compiler_params=pltpu.CompilerParams(
            collective_id=0, has_side_effects=True, vmem_limit_bytes=60 * 2**20
        ),
        name="sage_layer",
    )(*args)
    return pl.pallas_call(
        finish,
        out_shape=(
            jax.ShapeDtypeStruct((rows, width), BF16),
            jax.ShapeDtypeStruct((rows, width), BF16),
            jax.ShapeDtypeStruct((width, width), F32),
            jax.ShapeDtypeStruct((width, width), F32),
        ),
        in_specs=[any_space] * 3,
        out_specs=(any_space,) * 4,
        scratch_shapes=[
            vmem(rows, width), vmem(rows, width), vmem(2 * width, width), vmem(2 * width, width, dtype=F32),
            dma((2 + 2 * width // BLK,)), dma((2 + 2 * width // BLK,)),
        ],
        compiler_params=pltpu.CompilerParams(vmem_limit_bytes=60 * 2**20),
        name="finish",
    )(output, feature_grads, grads)


def solution(mesh):
    split = P(("dom", "rep"), None)
    split3 = P(("dom", "rep"), None, None)
    return jax.shard_map(
        functools.partial(body, mesh.shape["dom"], mesh.shape["rep"]),
        mesh=mesh,
        in_specs=(
            split, split, split3, split, split, split3, split, split, P(), P(), split,
        ),
        out_specs=(split, split, P(), P()),
        check_vma=False,
    )
```

```python
import functools
import math

import jax
import jax.numpy as jnp
from jax import lax
from jax.experimental import pallas as pl
from jax.experimental.pallas import tpu as pltpu
from jax.sharding import PartitionSpec as P

BLK = 128
MESH = pl.DeviceIdType.MESH
F32 = jnp.float32
BF16 = jnp.bfloat16


def dot(a, b):
    return jnp.dot(a, b, preferred_element_type=F32)


def dot_t(a, b):
    return lax.dot_general(a, b, (((0,), (0,)), ((), ())), preferred_element_type=F32)


def dot_nt(a, b):
    return lax.dot_general(a, b, (((1,), (1,)), ((), ())), preferred_element_type=F32)


def rows_at(start, size):
    return pl.ds(pl.multiple_of(start, size), size)


def kernel(
    domains, members, pieces, scale,
    feat_h, loc_h, rem_h, rdest_h, send_h, halo_h, hdest_h, exp_h, ws_h, wn_h, cot_h,
    out_h, fg_h, grads_h,
    pair, loc_v, rem_v, halo_v, ws_v, wn_v, cot_v, out_v, fg_v,
    rdest, send, hdest, export,
    outgoing, exported, arrived, beside, adj, acc, lin, lg, mg,
    mate_out, mate_in, own, xy_out, xy_in, z_out, z_in, grads,
    edge, returned, halo_edge, halo_back,
    in_sem, out_sem,
    f_send, f_recv, h_send, h_recv,
    m_send, m_recv, x_send, x_recv, z_send, z_recv,
    e_send, e_recv, b_send, b_recv,
    gz_send, gz_recv, gx_send, gx_recv, gm_send, gm_recv,
):
    dom = lax.axis_index("dom")
    me = lax.axis_index("rep")
    z = dom // 2
    core = dom % 2
    mate = dom + 1 - 2 * core
    zs = domains // 2
    rows, width = out_v.shape
    blocks = rows // BLK
    chunk = width // members
    piece = chunk // pieces
    relay = members == 4
    beside_x = me + 1 - 2 * (me % 2)
    beside_y = (me + 2) % 4
    across = 3 - me
    peers = [across, beside_x, beside_y] if relay else [(me + k) % members for k in range(1, members)]
    zpeers = [(z + k) % zs for k in range(1, zs)]
    has_prev = dom > 0
    has_next = dom < domains - 1
    sends = []

    def remote(src, dst, s_sem, r_sem, to):
        return pltpu.make_async_remote_copy(
            src_ref=src, dst_ref=dst, send_sem=s_sem, recv_sem=r_sem,
            device_id=to, device_id_type=MESH,
        )

    def push(*args):
        copy = remote(*args)
        copy.start()
        sends.append(copy)

    barrier = pltpu.get_barrier_semaphore()

    def greet(to):
        pl.semaphore_signal(barrier, inc=1, device_id=to, device_id_type=MESH)

    for q in peers:
        greet((dom, q))
    for j in zpeers:
        greet((j * 2 + core, me))
    greet((mate, me))
    outer = jnp.where(core == 0, dom - 1, dom + 1)
    has_outer = jnp.logical_and(outer >= 0, outer < domains)

    @pl.when(has_outer)
    def _():
        greet((outer, me))

    loads = {}
    for i, (name, src, dst) in enumerate([
        ("feat", feat_h, pair.at[0]), ("send", send_h, send), ("export", exp_h, export),
        ("rdest", rdest_h, rdest), ("hdest", hdest_h, hdest), ("loc", loc_h, loc_v),
        ("rem", rem_h, rem_v), ("halo", halo_h, halo_v), ("ws", ws_h, ws_v),
        ("wn", wn_h, wn_v), ("cot", cot_h, cot_v),
    ]):
        loads[name] = pltpu.make_async_copy(src, dst, in_sem.at[i])
        loads[name].start()

    for name in ("send", "export", "feat"):
        loads[name].wait()

    def picked(index):
        total = jnp.zeros((BLK, width), F32)
        for b in range(blocks):
            total = total + pair[0, b * BLK:(b + 1) * BLK, :].astype(F32) * (index == b).astype(F32)
        return total.astype(BF16)

    for q in peers:
        outgoing[rows_at(q * BLK, BLK), :] = picked(send[0, q])
    arrived[rows_at(me * BLK, BLK), :] = picked(send[0, me])
    exported[...] = picked(export[0, 0])

    pl.semaphore_wait(barrier, len(peers) + len(zpeers) + 1 + has_outer.astype(jnp.int32))

    for q in peers:
        push(
            outgoing.at[rows_at(q * BLK, BLK)], arrived.at[rows_at(me * BLK, BLK)],
            f_send.at[q], f_recv.at[me], (dom, q),
        )

    def exchange(sources, landing, s_sem, r_sem):
        to_prev = remote(sources[0], landing.at[pl.ds(BLK, BLK)], s_sem.at[0], r_sem.at[1], (dom - 1, me))
        to_next = remote(sources[1], landing.at[pl.ds(0, BLK)], s_sem.at[1], r_sem.at[0], (dom + 1, me))
        return to_prev, to_next

    def start_exchange(copies, landing):
        for slot, (there, copy) in enumerate(zip((has_prev, has_next), copies)):
            @pl.when(there)
            def _(copy=copy):
                copy.start()

            @pl.when(jnp.logical_not(there))
            def _(slot=slot):
                landing[pl.ds(slot * BLK, BLK), :] = jnp.zeros((BLK, width), BF16)

    def arrive_exchange(copies):
        to_prev, to_next = copies

        @pl.when(has_prev)
        def _():
            to_next.wait_recv()

        @pl.when(has_next)
        def _():
            to_prev.wait_recv()

    def end_exchange(copies):
        for there, copy in zip((has_prev, has_next), copies):
            @pl.when(there)
            def _(copy=copy):
                copy.wait_send()

    halo_f = exchange((exported, exported), beside, h_send, h_recv)
    start_exchange(halo_f, beside)

    for name in ("rdest", "hdest", "loc", "rem", "halo"):
        loads[name].wait()
    counts = loc_v[...].astype(F32)
    adj[:, :rows] = counts.astype(BF16)
    local_degree = jnp.sum(counts, axis=1, keepdims=True)
    for b in range(blocks):
        total = jnp.zeros((BLK, BLK), F32)
        for q in range(members + 2):
            if q < members:
                here = (rdest[0, q] == b).astype(F32)
                placed = rem_v[q].astype(F32) * here
            else:
                here = (hdest[0, q - members] == b).astype(F32)
                placed = halo_v[q - members].astype(F32) * here
            total = total + placed
            adj[b * BLK:(b + 1) * BLK, rows + q * BLK:rows + (q + 1) * BLK] = placed.astype(BF16)
        degree = jnp.sum(total, axis=1, keepdims=True) + local_degree[b * BLK:(b + 1) * BLK]
        acc[b * BLK:(b + 1) * BLK, :BLK] = jnp.broadcast_to(1.0 / jnp.maximum(degree, 1.0), (BLK, BLK))
    inverse = acc[:, :1]

    acc[...] = dot(adj[:, :rows], pair[0])
    loads["ws"].wait()
    lin[...] = dot(pair[0], ws_v[...])
    loads["wn"].wait()
    loads["cot"].wait()
    arrive_exchange(halo_f)
    acc[...] += dot(adj[:, rows + members * BLK:], beside[...])
    for q in peers:
        slot = arrived.at[rows_at(q * BLK, BLK)]
        remote(slot, slot, f_send.at[q], f_recv.at[q], (dom, q)).wait_recv()
    mean = (acc[...] + dot(adj[:, rows:rows + members * BLK], arrived[...])) * inverse
    pair[1] = mean.astype(BF16)

    x = lin[...] + dot(pair[1], wn_v[...])
    c = math.sqrt(2.0 / math.pi)
    square = x * x
    t = jnp.tanh(c * (x + 0.044715 * (x * square)))
    half = 0.5 * (1.0 + t)
    out_v[...] = (x * half).astype(BF16)
    slope = half + 0.5 * x * (1.0 - t * t) * (c * (1.0 + 3.0 * 0.044715 * square))
    lg[...] = (cot_v[...].astype(F32) * slope).astype(BF16)
    out_copy = pltpu.make_async_copy(out_v, out_h, out_sem.at[0])
    out_copy.start()

    layer = members * piece
    parts = [(z + k) % zs for k in range(1, zs)] + [z] if pieces > 1 else [0]
    mine = parts[-1]
    mate_out[...] = dot_t(pair[1 - core], lg[...]).astype(BF16)

    def mate_copy(j):
        at = rows_at(j * layer, layer)
        return mate_out.at[at], mate_in.at[at], m_send.at[j], m_recv.at[j], (mate, me)

    for j in parts:
        push(*mate_copy(j))
    own[...] = dot_t(pair[core], lg[...])
    for n, j in enumerate(parts):
        remote(*mate_copy(j)).wait_recv()
        at = rows_at(j * layer, layer)
        own[at, :] += mate_in[at, :].astype(F32)
        xy_out[at, :] = own[at, :].astype(BF16)
        for q in peers:
            push(
                xy_out.at[rows_at(j * layer + q * piece, piece)],
                xy_in.at[rows_at((me * pieces + j) * piece, piece)],
                x_send.at[q * pieces + j], x_recv.at[me * pieces + j], (dom, q),
            )

    mg[...] = (dot_nt(lg[...], wn_v[...]) * inverse).astype(BF16)
    edge[...] = dot_t(adj[:, rows:rows + members * BLK], mg[...]).astype(BF16)
    halo_edge[...] = dot_t(adj[:, rows + members * BLK:], mg[...]).astype(BF16)
    returned[rows_at(me * BLK, BLK), :] = edge[rows_at(me * BLK, BLK), :]
    halo_b = exchange((halo_edge.at[pl.ds(0, BLK)], halo_edge.at[pl.ds(BLK, BLK)]), halo_back, b_send, b_recv)
    start_exchange(halo_b, halo_back)

    def z_slot(j):
        return z_in.at[rows_at(j * piece, piece)]

    for j in parts:
        total = own[rows_at(j * layer + me * piece, piece), :]
        for q in peers:
            slot = rows_at((q * pieces + j) * piece, piece)
            remote(
                xy_in.at[slot], xy_in.at[slot],
                x_send.at[q * pieces + j], x_recv.at[q * pieces + j], (dom, q),
            ).wait_recv()
            total = total + xy_in[slot, :].astype(F32)
        total = total.astype(BF16)
        targets = [j] if pieces > 1 else zpeers
        if pieces == 1 or j is not mine:
            for to in targets:
                out = rows_at(to * piece, piece)
                z_out[out, :] = total
                push(z_out.at[out], z_slot(z), z_send.at[to], z_recv.at[z], (to * 2 + core, me))
        if j is mine:
            z_in[rows_at(z * piece, piece), :] = total
    for q in peers:
        push(
            edge.at[rows_at(q * BLK, BLK)], returned.at[rows_at(me * BLK, BLK)],
            e_send.at[q], e_recv.at[me], (dom, q),
        )
    acc[...] = dot_nt(lg[...], ws_v[...]) + dot_t(adj[:, :rows], mg[...])
    for j in zpeers:
        remote(z_slot(j), z_slot(j), z_send.at[j], z_recv.at[j], (j * 2 + core, me)).wait_recv()
    total = z_in[:piece, :].astype(F32)
    for j in range(1, zs):
        total = total + z_in[j * piece:(j + 1) * piece, :].astype(F32)

    def place(member, part, half=core):
        return rows_at(half * width + part * layer + member * piece, piece)

    grads[place(me, mine), :] = (total * scale).astype(BF16)

    def to_mate(member, j):
        at = grads.at[place(member, j)]
        push(at, at, gm_send.at[member * pieces + j], gm_recv.at[member * pieces + j], (mate, me))

    def to_peer(q, member, j):
        at = grads.at[place(member, j)]
        push(at, at, gx_send.at[q * pieces + j], gx_recv.at[member * pieces + j], (dom, q))

    def from_peer(member, j):
        at = grads.at[place(member, j)]
        remote(at, at, gx_send.at[member * pieces + j], gx_recv.at[member * pieces + j], (dom, member)).wait_recv()

    direct = [beside_x, beside_y] if relay else peers

    def spread(j):
        for q in direct:
            to_peer(q, me, j)
        to_mate(me, j)

    if pieces > 1:
        at = grads.at[place(me, z)]
        for j in zpeers:
            push(at, at, gz_send.at[j], gz_recv.at[z], (j * 2 + core, me))
    spread(mine)
    if pieces > 1:
        for j in zpeers:
            at = grads.at[place(me, j)]
            remote(at, at, gz_send.at[j], gz_recv.at[j], (j * 2 + core, me)).wait_recv()
            spread(j)

    arrivals = [mine] + (zpeers if pieces > 1 else [])
    for j in arrivals:
        for q in direct:
            from_peer(q, j)
        if relay:
            first = j % 2
            source = beside_x * (1 - first) + beside_y * first
            to_peer(beside_x + beside_y - source, source, j)
        for q in direct:
            to_mate(q, j)

    if relay:
        for j in arrivals:
            from_peer(across, j)
            to_mate(across, j)
    arrive_exchange(halo_b)
    for q in peers:
        slot = returned.at[rows_at(q * BLK, BLK)]
        remote(slot, slot, e_send.at[q], e_recv.at[q], (dom, q)).wait_recv()
    incoming = halo_back[:BLK, :].astype(F32) + halo_back[BLK:, :].astype(F32)
    for b in range(blocks):
        total = acc[b * BLK:(b + 1) * BLK, :] + incoming * (export[0, 0] == b).astype(F32)
        for q in range(members):
            back = returned[q * BLK:(q + 1) * BLK, :].astype(F32)
            total = total + back * (send[0, q] == b).astype(F32)
        fg_v[b * BLK:(b + 1) * BLK, :] = total.astype(BF16)
    fg_copy = pltpu.make_async_copy(fg_v, fg_h, out_sem.at[1])
    fg_copy.start()

    writes = []

    def write(half, j):
        at = rows_at(half * width + j * layer, layer)
        copy = pltpu.make_async_copy(grads.at[at], grads_h.at[at], out_sem.at[2 + len(writes)])
        copy.start()
        writes.append(copy)

    for j in arrivals:
        write(core, j)
    for j in arrivals:
        for q in [me] + peers:
            at = grads.at[place(q, j, 1 - core)]
            remote(at, at, gm_send.at[q * pieces + j], gm_recv.at[q * pieces + j], (mate, me)).wait_recv()
        write(1 - core, j)

    for copy in sends:
        copy.wait_send()
    end_exchange(halo_f)
    end_exchange(halo_b)
    out_copy.wait()
    fg_copy.wait()
    for copy in writes:
        copy.wait()


def finish(out_i, fg_i, grads_i, out_o, fg_o, self_o, neigh_o, out_v, fg_v, narrow, wide, load_sem, sem):
    width = self_o.shape[0]
    starts = range(0, 2 * width, BLK)
    loads = [
        pltpu.make_async_copy(grads_i.at[pl.ds(start, BLK)], narrow.at[pl.ds(start, BLK)], load_sem.at[2 + n])
        for n, start in enumerate(starts)
    ]
    loads += [
        pltpu.make_async_copy(out_i, out_v, load_sem.at[0]),
        pltpu.make_async_copy(fg_i, fg_v, load_sem.at[1]),
    ]
    for copy in loads:
        copy.start()
    stores = []
    for n, start in enumerate(starts):
        at = pl.ds(start, BLK)
        loads[n].wait()
        wide[at, :] = narrow[at, :].astype(F32)
        dst = self_o if start < width else neigh_o
        stores.append(pltpu.make_async_copy(wide.at[at], dst.at[pl.ds(start % width, BLK)], sem.at[2 + n]))
        stores[-1].start()
    for n, (src, dst) in enumerate(((out_v, out_o), (fg_v, fg_o))):
        loads[n - 2].wait()
        stores.append(pltpu.make_async_copy(src, dst, sem.at[n]))
        stores[-1].start()
    for copy in stores:
        copy.wait()


def body(domains, members, *args):
    features, w_self = args[0], args[8]
    rows, width = features.shape
    zs = domains // 2
    chunk = width // members
    pieces = zs if chunk % (16 * zs) == 0 else 1
    piece = chunk // pieces
    scale = 1.0 / math.sqrt(rows * members * domains)
    any_space = pl.BlockSpec(memory_space=pl.ANY)
    dma = pltpu.SemaphoreType.DMA

    def vmem(*shape, dtype=BF16):
        return pltpu.VMEM(shape, dtype)

    scratch = [
        vmem(2, rows, width),
        vmem(rows, rows, dtype=jnp.int32),
        vmem(members, BLK, BLK, dtype=jnp.int32),
        vmem(2, BLK, BLK, dtype=jnp.int32),
        vmem(width, width), vmem(width, width), vmem(rows, width),
        vmem(rows, width), vmem(rows, width),
        pltpu.SMEM((1, members), jnp.int32), pltpu.SMEM((1, members), jnp.int32),
        pltpu.SMEM((1, 2), jnp.int32), pltpu.SMEM((1, 1), jnp.int32),
        vmem(members * BLK, width), vmem(BLK, width), vmem(members * BLK, width), vmem(2 * BLK, width),
        vmem(rows, rows + (members + 2) * BLK),
        vmem(rows, width, dtype=F32), vmem(rows, width, dtype=F32),
        vmem(rows, width), vmem(rows, width),
        vmem(width, width), vmem(width, width), vmem(width, width, dtype=F32),
        vmem(width, width), vmem(width, width),
        vmem(zs * piece, width), vmem(zs * piece, width), vmem(2 * width, width),
        vmem(members * BLK, width), vmem(members * BLK, width), vmem(2 * BLK, width), vmem(2 * BLK, width),
        dma((11,)), dma((2 + 2 * pieces,)),
        dma((members,)), dma((members,)), dma((2,)), dma((2,)),
        dma((pieces,)), dma((pieces,)), dma((members * pieces,)), dma((members * pieces,)), dma((zs,)), dma((zs,)),
        dma((members,)), dma((members,)), dma((2,)), dma((2,)),
        dma((zs,)), dma((zs,)),
        dma((members * pieces,)), dma((members * pieces,)), dma((members * pieces,)), dma((members * pieces,)),
    ]
    output, feature_grads, grads = pl.pallas_call(
        functools.partial(kernel, domains, members, pieces, scale),
        out_shape=(
            jax.ShapeDtypeStruct((rows, width), BF16),
            jax.ShapeDtypeStruct((rows, width), BF16),
            jax.ShapeDtypeStruct((2 * width, width), BF16),
        ),
        in_specs=[any_space] * len(args),
        out_specs=(any_space,) * 3,
        scratch_shapes=scratch,
        compiler_params=pltpu.CompilerParams(
            collective_id=0, has_side_effects=True, vmem_limit_bytes=60 * 2**20
        ),
        name="sage_layer",
    )(*args)
    return pl.pallas_call(
        finish,
        out_shape=(
            jax.ShapeDtypeStruct((rows, width), BF16),
            jax.ShapeDtypeStruct((rows, width), BF16),
            jax.ShapeDtypeStruct((width, width), F32),
            jax.ShapeDtypeStruct((width, width), F32),
        ),
        in_specs=[any_space] * 3,
        out_specs=(any_space,) * 4,
        scratch_shapes=[
            vmem(rows, width), vmem(rows, width), vmem(2 * width, width), vmem(2 * width, width, dtype=F32),
            dma((2 + 2 * width // BLK,)), dma((2 + 2 * width // BLK,)),
        ],
        compiler_params=pltpu.CompilerParams(vmem_limit_bytes=60 * 2**20),
        name="finish",
    )(output, feature_grads, grads)


def solution(mesh):
    split = P(("dom", "rep"), None)
    split3 = P(("dom", "rep"), None, None)
    return jax.shard_map(
        functools.partial(body, mesh.shape["dom"], mesh.shape["rep"]),
        mesh=mesh,
        in_specs=(
            split, split, split3, split, split, split3, split, split, P(), P(), split,
        ),
        out_specs=(split, split, P(), P()),
        check_vma=False,
    )
```

```python
import functools
import math

import jax
import jax.numpy as jnp
from jax import lax
from jax.experimental import pallas as pl
from jax.experimental.pallas import tpu as pltpu
from jax.sharding import PartitionSpec as P

BLK = 128
MESH = pl.DeviceIdType.MESH
F32 = jnp.float32
BF16 = jnp.bfloat16


def dot(a, b):
    return jnp.dot(a, b, preferred_element_type=F32)


def dot_t(a, b):
    return lax.dot_general(a, b, (((0,), (0,)), ((), ())), preferred_element_type=F32)


def dot_nt(a, b):
    return lax.dot_general(a, b, (((1,), (1,)), ((), ())), preferred_element_type=F32)


def rows_at(start, size):
    return pl.ds(pl.multiple_of(start, size), size)


def kernel(
    domains, members, pieces, scale,
    feat_h, loc_h, rem_h, rdest_h, send_h, halo_h, hdest_h, exp_h, ws_h, wn_h, cot_h,
    out_h, fg_h, grads_h,
    pair, loc_v, rem_v, halo_v, ws_v, wn_v, cot_v, out_v, fg_v,
    rdest, send, hdest, export,
    outgoing, exported, arrived, beside, adj, acc, lin, lg, mg,
    mate_out, mate_in, own, xy_out, xy_in, z_out, z_in, grads,
    edge, returned, halo_edge, halo_back,
    in_sem, out_sem,
    f_send, f_recv, h_send, h_recv,
    m_send, m_recv, x_send, x_recv, z_send, z_recv,
    e_send, e_recv, b_send, b_recv,
    gz_send, gz_recv, gx_send, gx_recv, gm_send, gm_recv,
):
    dom = lax.axis_index("dom")
    me = lax.axis_index("rep")
    z = dom // 2
    core = dom % 2
    mate = dom + 1 - 2 * core
    zs = domains // 2
    rows, width = out_v.shape
    blocks = rows // BLK
    chunk = width // members
    piece = chunk // pieces
    beside_x = me + 1 - 2 * (me % 2)
    beside_y = (me + 2) % 4
    across = 3 - me
    peers = [across, beside_x, beside_y] if members == 4 else [(me + k) % members for k in range(1, members)]
    zpeers = [(z + k) % zs for k in range(1, zs)]
    has_prev = dom > 0
    has_next = dom < domains - 1
    sends = []

    def remote(src, dst, s_sem, r_sem, to):
        return pltpu.make_async_remote_copy(
            src_ref=src, dst_ref=dst, send_sem=s_sem, recv_sem=r_sem,
            device_id=to, device_id_type=MESH,
        )

    def push(*args):
        copy = remote(*args)
        copy.start()
        sends.append(copy)

    barrier = pltpu.get_barrier_semaphore()

    def greet(to):
        pl.semaphore_signal(barrier, inc=1, device_id=to, device_id_type=MESH)

    for q in peers:
        greet((dom, q))
    for j in zpeers:
        greet((j * 2 + core, me))
    greet((mate, me))
    outer = jnp.where(core == 0, dom - 1, dom + 1)
    has_outer = jnp.logical_and(outer >= 0, outer < domains)

    @pl.when(has_outer)
    def _():
        greet((outer, me))

    loads = {}
    for i, (name, src, dst) in enumerate([
        ("feat", feat_h, pair.at[0]), ("send", send_h, send), ("export", exp_h, export),
        ("rdest", rdest_h, rdest), ("hdest", hdest_h, hdest), ("loc", loc_h, loc_v),
        ("rem", rem_h, rem_v), ("halo", halo_h, halo_v), ("ws", ws_h, ws_v),
        ("wn", wn_h, wn_v), ("cot", cot_h, cot_v),
    ]):
        loads[name] = pltpu.make_async_copy(src, dst, in_sem.at[i])
        loads[name].start()

    for name in ("send", "export", "feat"):
        loads[name].wait()

    def picked(index):
        total = jnp.zeros((BLK, width), F32)
        for b in range(blocks):
            total = total + pair[0, b * BLK:(b + 1) * BLK, :].astype(F32) * (index == b).astype(F32)
        return total.astype(BF16)

    for q in peers:
        outgoing[rows_at(q * BLK, BLK), :] = picked(send[0, q])
    arrived[rows_at(me * BLK, BLK), :] = picked(send[0, me])
    exported[...] = picked(export[0, 0])

    pl.semaphore_wait(barrier, len(peers) + len(zpeers) + 1 + has_outer.astype(jnp.int32))

    for q in peers:
        push(
            outgoing.at[rows_at(q * BLK, BLK)], arrived.at[rows_at(me * BLK, BLK)],
            f_send.at[q], f_recv.at[me], (dom, q),
        )

    def exchange(sources, landing, s_sem, r_sem):
        to_prev = remote(sources[0], landing.at[pl.ds(BLK, BLK)], s_sem.at[0], r_sem.at[1], (dom - 1, me))
        to_next = remote(sources[1], landing.at[pl.ds(0, BLK)], s_sem.at[1], r_sem.at[0], (dom + 1, me))
        return to_prev, to_next

    def start_exchange(copies, landing):
        for slot, (there, copy) in enumerate(zip((has_prev, has_next), copies)):
            @pl.when(there)
            def _(copy=copy):
                copy.start()

            @pl.when(jnp.logical_not(there))
            def _(slot=slot):
                landing[pl.ds(slot * BLK, BLK), :] = jnp.zeros((BLK, width), BF16)

    def arrive_exchange(copies):
        to_prev, to_next = copies

        @pl.when(has_prev)
        def _():
            to_next.wait_recv()

        @pl.when(has_next)
        def _():
            to_prev.wait_recv()

    def end_exchange(copies):
        for there, copy in zip((has_prev, has_next), copies):
            @pl.when(there)
            def _(copy=copy):
                copy.wait_send()

    halo_f = exchange((exported, exported), beside, h_send, h_recv)
    start_exchange(halo_f, beside)

    for name in ("rdest", "hdest", "loc", "rem", "halo"):
        loads[name].wait()
    counts = loc_v[...].astype(F32)
    adj[:, :rows] = counts.astype(BF16)
    local_degree = jnp.sum(counts, axis=1, keepdims=True)
    for b in range(blocks):
        total = jnp.zeros((BLK, BLK), F32)
        for q in range(members + 2):
            if q < members:
                here = (rdest[0, q] == b).astype(F32)
                placed = rem_v[q].astype(F32) * here
            else:
                here = (hdest[0, q - members] == b).astype(F32)
                placed = halo_v[q - members].astype(F32) * here
            total = total + placed
            adj[b * BLK:(b + 1) * BLK, rows + q * BLK:rows + (q + 1) * BLK] = placed.astype(BF16)
        degree = jnp.sum(total, axis=1, keepdims=True) + local_degree[b * BLK:(b + 1) * BLK]
        acc[b * BLK:(b + 1) * BLK, :BLK] = jnp.broadcast_to(1.0 / jnp.maximum(degree, 1.0), (BLK, BLK))
    inverse = acc[:, :1]

    acc[...] = dot(adj[:, :rows], pair[0])
    loads["ws"].wait()
    lin[...] = dot(pair[0], ws_v[...])
    loads["wn"].wait()
    loads["cot"].wait()
    arrive_exchange(halo_f)
    acc[...] += dot(adj[:, rows + members * BLK:], beside[...])
    for q in peers:
        slot = arrived.at[rows_at(q * BLK, BLK)]
        remote(slot, slot, f_send.at[q], f_recv.at[q], (dom, q)).wait_recv()
    mean = (acc[...] + dot(adj[:, rows:rows + members * BLK], arrived[...])) * inverse
    pair[1] = mean.astype(BF16)

    x = lin[...] + dot(pair[1], wn_v[...])
    c = math.sqrt(2.0 / math.pi)
    square = x * x
    t = jnp.tanh(c * (x + 0.044715 * (x * square)))
    half = 0.5 * (1.0 + t)
    out_v[...] = (x * half).astype(BF16)
    slope = half + 0.5 * x * (1.0 - t * t) * (c * (1.0 + 3.0 * 0.044715 * square))
    lg[...] = (cot_v[...].astype(F32) * slope).astype(BF16)
    out_copy = pltpu.make_async_copy(out_v, out_h, out_sem.at[0])
    out_copy.start()

    layer = members * piece
    parts = [(z + k) % zs for k in range(1, zs)] + [z] if pieces > 1 else [0]
    mine = parts[-1]
    mate_out[...] = dot_t(pair[1 - core], lg[...]).astype(BF16)

    def mate_copy(j):
        at = rows_at(j * layer, layer)
        return mate_out.at[at], mate_in.at[at], m_send.at[j], m_recv.at[j], (mate, me)

    for j in parts:
        push(*mate_copy(j))
    own[...] = dot_t(pair[core], lg[...])
    for n, j in enumerate(parts):
        remote(*mate_copy(j)).wait_recv()
        at = rows_at(j * layer, layer)
        own[at, :] += mate_in[at, :].astype(F32)
        xy_out[at, :] = own[at, :].astype(BF16)
        for q in peers:
            push(
                xy_out.at[rows_at(j * layer + q * piece, piece)],
                xy_in.at[rows_at((me * pieces + j) * piece, piece)],
                x_send.at[q * pieces + j], x_recv.at[me * pieces + j], (dom, q),
            )

    mg[...] = (dot_nt(lg[...], wn_v[...]) * inverse).astype(BF16)
    edge[...] = dot_t(adj[:, rows:rows + members * BLK], mg[...]).astype(BF16)
    halo_edge[...] = dot_t(adj[:, rows + members * BLK:], mg[...]).astype(BF16)
    returned[rows_at(me * BLK, BLK), :] = edge[rows_at(me * BLK, BLK), :]
    halo_b = exchange((halo_edge.at[pl.ds(0, BLK)], halo_edge.at[pl.ds(BLK, BLK)]), halo_back, b_send, b_recv)
    start_exchange(halo_b, halo_back)

    def z_slot(j):
        return z_in.at[rows_at(j * piece, piece)]

    for j in parts:
        total = own[rows_at(j * layer + me * piece, piece), :]
        for q in peers:
            slot = rows_at((q * pieces + j) * piece, piece)
            remote(
                xy_in.at[slot], xy_in.at[slot],
                x_send.at[q * pieces + j], x_recv.at[q * pieces + j], (dom, q),
            ).wait_recv()
            total = total + xy_in[slot, :].astype(F32)
        total = total.astype(BF16)
        targets = [j] if pieces > 1 else zpeers
        if pieces == 1 or j is not mine:
            for to in targets:
                out = rows_at(to * piece, piece)
                z_out[out, :] = total
                push(z_out.at[out], z_slot(z), z_send.at[to], z_recv.at[z], (to * 2 + core, me))
        if j is mine:
            z_in[rows_at(z * piece, piece), :] = total
    for q in peers:
        push(
            edge.at[rows_at(q * BLK, BLK)], returned.at[rows_at(me * BLK, BLK)],
            e_send.at[q], e_recv.at[me], (dom, q),
        )
    acc[...] = dot_nt(lg[...], ws_v[...]) + dot_t(adj[:, :rows], mg[...])
    for j in zpeers:
        remote(z_slot(j), z_slot(j), z_send.at[j], z_recv.at[j], (j * 2 + core, me)).wait_recv()
    total = z_in[:piece, :].astype(F32)
    for j in range(1, zs):
        total = total + z_in[j * piece:(j + 1) * piece, :].astype(F32)

    def place(member, part, half=core):
        return rows_at(half * width + part * layer + member * piece, piece)

    grads[place(me, mine), :] = (total * scale).astype(BF16)

    def to_mate(member, j):
        at = grads.at[place(member, j)]
        push(at, at, gm_send.at[member * pieces + j], gm_recv.at[member * pieces + j], (mate, me))

    def to_peer(q, member, j):
        at = grads.at[place(member, j)]
        push(at, at, gx_send.at[q * pieces + j], gx_recv.at[member * pieces + j], (dom, q))

    def from_peer(member, j):
        at = grads.at[place(member, j)]
        remote(at, at, gx_send.at[member * pieces + j], gx_recv.at[member * pieces + j], (dom, member)).wait_recv()


    def spread(j):
        for q in peers:
            to_peer(q, me, j)
        to_mate(me, j)

    if pieces > 1:
        at = grads.at[place(me, z)]
        for j in zpeers:
            push(at, at, gz_send.at[j], gz_recv.at[z], (j * 2 + core, me))
    spread(mine)
    if pieces > 1:
        for j in zpeers:
            at = grads.at[place(me, j)]
            remote(at, at, gz_send.at[j], gz_recv.at[j], (j * 2 + core, me)).wait_recv()
            spread(j)

    arrivals = [mine] + (zpeers if pieces > 1 else [])
    for j in arrivals:
        for q in peers:
            from_peer(q, j)
        for q in peers:
            to_mate(q, j)

    arrive_exchange(halo_b)
    for q in peers:
        slot = returned.at[rows_at(q * BLK, BLK)]
        remote(slot, slot, e_send.at[q], e_recv.at[q], (dom, q)).wait_recv()
    incoming = halo_back[:BLK, :].astype(F32) + halo_back[BLK:, :].astype(F32)
    for b in range(blocks):
        total = acc[b * BLK:(b + 1) * BLK, :] + incoming * (export[0, 0] == b).astype(F32)
        for q in range(members):
            back = returned[q * BLK:(q + 1) * BLK, :].astype(F32)
            total = total + back * (send[0, q] == b).astype(F32)
        fg_v[b * BLK:(b + 1) * BLK, :] = total.astype(BF16)
    fg_copy = pltpu.make_async_copy(fg_v, fg_h, out_sem.at[1])
    fg_copy.start()

    writes = []

    def write(half, j):
        at = rows_at(half * width + j * layer, layer)
        copy = pltpu.make_async_copy(grads.at[at], grads_h.at[at], out_sem.at[2 + len(writes)])
        copy.start()
        writes.append(copy)

    for j in arrivals:
        write(core, j)
    for j in arrivals:
        for q in [me] + peers:
            at = grads.at[place(q, j, 1 - core)]
            remote(at, at, gm_send.at[q * pieces + j], gm_recv.at[q * pieces + j], (mate, me)).wait_recv()
        write(1 - core, j)

    for copy in sends:
        copy.wait_send()
    end_exchange(halo_f)
    end_exchange(halo_b)
    out_copy.wait()
    fg_copy.wait()
    for copy in writes:
        copy.wait()


def finish(out_i, fg_i, grads_i, out_o, fg_o, self_o, neigh_o, out_v, fg_v, narrow, wide, load_sem, sem):
    width = self_o.shape[0]
    starts = range(0, 2 * width, BLK)
    loads = [
        pltpu.make_async_copy(grads_i.at[pl.ds(start, BLK)], narrow.at[pl.ds(start, BLK)], load_sem.at[2 + n])
        for n, start in enumerate(starts)
    ]
    loads += [
        pltpu.make_async_copy(out_i, out_v, load_sem.at[0]),
        pltpu.make_async_copy(fg_i, fg_v, load_sem.at[1]),
    ]
    for copy in loads:
        copy.start()
    stores = []
    for n, start in enumerate(starts):
        at = pl.ds(start, BLK)
        loads[n].wait()
        wide[at, :] = narrow[at, :].astype(F32)
        dst = self_o if start < width else neigh_o
        stores.append(pltpu.make_async_copy(wide.at[at], dst.at[pl.ds(start % width, BLK)], sem.at[2 + n]))
        stores[-1].start()
    for n, (src, dst) in enumerate(((out_v, out_o), (fg_v, fg_o))):
        loads[n - 2].wait()
        stores.append(pltpu.make_async_copy(src, dst, sem.at[n]))
        stores[-1].start()
    for copy in stores:
        copy.wait()


def body(domains, members, *args):
    features, w_self = args[0], args[8]
    rows, width = features.shape
    zs = domains // 2
    chunk = width // members
    pieces = zs if chunk % (16 * zs) == 0 else 1
    piece = chunk // pieces
    scale = 1.0 / math.sqrt(rows * members * domains)
    any_space = pl.BlockSpec(memory_space=pl.ANY)
    dma = pltpu.SemaphoreType.DMA

    def vmem(*shape, dtype=BF16):
        return pltpu.VMEM(shape, dtype)

    scratch = [
        vmem(2, rows, width),
        vmem(rows, rows, dtype=jnp.int32),
        vmem(members, BLK, BLK, dtype=jnp.int32),
        vmem(2, BLK, BLK, dtype=jnp.int32),
        vmem(width, width), vmem(width, width), vmem(rows, width),
        vmem(rows, width), vmem(rows, width),
        pltpu.SMEM((1, members), jnp.int32), pltpu.SMEM((1, members), jnp.int32),
        pltpu.SMEM((1, 2), jnp.int32), pltpu.SMEM((1, 1), jnp.int32),
        vmem(members * BLK, width), vmem(BLK, width), vmem(members * BLK, width), vmem(2 * BLK, width),
        vmem(rows, rows + (members + 2) * BLK),
        vmem(rows, width, dtype=F32), vmem(rows, width, dtype=F32),
        vmem(rows, width), vmem(rows, width),
        vmem(width, width), vmem(width, width), vmem(width, width, dtype=F32),
        vmem(width, width), vmem(width, width),
        vmem(zs * piece, width), vmem(zs * piece, width), vmem(2 * width, width),
        vmem(members * BLK, width), vmem(members * BLK, width), vmem(2 * BLK, width), vmem(2 * BLK, width),
        dma((11,)), dma((2 + 2 * pieces,)),
        dma((members,)), dma((members,)), dma((2,)), dma((2,)),
        dma((pieces,)), dma((pieces,)), dma((members * pieces,)), dma((members * pieces,)), dma((zs,)), dma((zs,)),
        dma((members,)), dma((members,)), dma((2,)), dma((2,)),
        dma((zs,)), dma((zs,)),
        dma((members * pieces,)), dma((members * pieces,)), dma((members * pieces,)), dma((members * pieces,)),
    ]
    output, feature_grads, grads = pl.pallas_call(
        functools.partial(kernel, domains, members, pieces, scale),
        out_shape=(
            jax.ShapeDtypeStruct((rows, width), BF16),
            jax.ShapeDtypeStruct((rows, width), BF16),
            jax.ShapeDtypeStruct((2 * width, width), BF16),
        ),
        in_specs=[any_space] * len(args),
        out_specs=(any_space,) * 3,
        scratch_shapes=scratch,
        compiler_params=pltpu.CompilerParams(
            collective_id=0, has_side_effects=True, vmem_limit_bytes=60 * 2**20
        ),
        name="sage_layer",
    )(*args)
    return pl.pallas_call(
        finish,
        out_shape=(
            jax.ShapeDtypeStruct((rows, width), BF16),
            jax.ShapeDtypeStruct((rows, width), BF16),
            jax.ShapeDtypeStruct((width, width), F32),
            jax.ShapeDtypeStruct((width, width), F32),
        ),
        in_specs=[any_space] * 3,
        out_specs=(any_space,) * 4,
        scratch_shapes=[
            vmem(rows, width), vmem(rows, width), vmem(2 * width, width), vmem(2 * width, width, dtype=F32),
            dma((2 + 2 * width // BLK,)), dma((2 + 2 * width // BLK,)),
        ],
        compiler_params=pltpu.CompilerParams(vmem_limit_bytes=60 * 2**20),
        name="finish",
    )(output, feature_grads, grads)


def solution(mesh):
    split = P(("dom", "rep"), None)
    split3 = P(("dom", "rep"), None, None)
    return jax.shard_map(
        functools.partial(body, mesh.shape["dom"], mesh.shape["rep"]),
        mesh=mesh,
        in_specs=(
            split, split, split3, split, split, split3, split, split, P(), P(), split,
        ),
        out_specs=(split, split, P(), P()),
        check_vma=False,
    )
```
